128 devices in a mesh: brick: 8 (over y, core), col: 16 (over z, x).
Axes of the slice: x: 4, y: 4, z: 4, core: 2. Of those that a mesh axis runs over, the one named last changes fastest.
Arguments:
- velocity: float32 [3, 256, 512, 128], P(None, 'brick', 'col'), may hold values from -6 to 6
- pressure: float32 [256, 512, 128], P('brick', 'col'), may hold values from -12 to 12
- level_set: float32 [256, 512, 128], P('brick', 'col'), may hold values from -12 to 12
- overset: int32 [256, 512, 128], P('brick', 'col'), may hold values from 0 to 2
- band_count: int32 [8, 16], P('brick', 'col'), may hold values from 1 to 16, 112 in all within a row
- band_ids: int32 [8, 16, 32], P('brick', 'col'), may hold values from 0 to 31, each once within a row
Outputs:
- velocity_star: float32 [3, 256, 512, 128], P(None, 'brick', 'col')
- level_set_new: float32 [256, 512, 128], P('brick', 'col')
The draws below stay inside these ranges and needn't reach their ends.
Inputs may be any that keep to these rules, and one draw needn't show every extreme that they name: `band_count`: in each brick row the counts over col sum to exactly 7 times the size of col; some device holds exactly 16. `band_ids`: each device's entries are a permutation of its 32 block numbers.
All inputs are finite; a program needn't handle non-finite values.
Results may differ from the reference program's by a relative error of at most 0.0003.
Values sent between devices are 32-bit elements; how exact they have to be, the bound alone decides.
No kernel may reach another device: no remote copies, remote signals or barrier semaphores. Data moves between devices by JAX's collectives and lax.ppermute only.
A program may use at most 320 MiB of HBM per device.

```python
import math
import jax
import jax.numpy as jnp
import numpy as np
from jax import lax

CX = 32
CY = 32
CZ = 128
BS = 16
REINIT = 3
MAXB = 16
BAND_DEV = 7
RIM = 4
CUBE = 24
BLK_DEV = 32
NX = 256
NY = 512
NZ = 128
N_BRICK = 8
N_COL = 16


def draw_overset(key, part):
    key = jax.random.fold_in(key, 7)
    marks = jax.random.randint(key, (NX, NY, NZ), 0, 20)
    return jnp.where(marks < 16, 0, jnp.where(marks < 19, 1, 2)).astype(jnp.int32)


def block_levels(key, shape, shards, smallest, high):
    level, own = 1.0, jax.random.fold_in(key, 6)
    for dim, blocks in shards:
        steps = jnp.exp(jax.random.uniform(jax.random.fold_in(own, dim), (blocks,), jnp.float32, smallest / len(shards), high / len(shards)))
        level = level * jnp.repeat(steps, shape[dim] // blocks).reshape([-1 if axis == dim else 1 for axis in range(len(shape))])
    return level


def split_up(count, total, reach, skew):
    portions = [(1 << 20) // math.isqrt(standing ** skew) + 1 for standing in range(2, count + 1)]
    spare, holding = total - reach - (count - 1), [1] * (count - 1)
    while spare > 0:
        movable = [i for i in range(count - 1) if holding[i] < reach]
        mass, left = sum([portions[i] for i in movable]), spare
        for i in movable:
            more = min(reach - holding[i], max(1, left * portions[i] // mass), spare)
            holding[i] = holding[i] + more
            spare = spare - more
    return np.array([reach] + holding)


def uneven_parts(stream_key, amount, total, reach, lean):
    if amount == 2:
        one = jax.random.randint(stream_key, (), max(1, total - reach), min(reach, total - 1) + 1)
        return jnp.stack([one, total - one])
    tallies = jnp.asarray(split_up(amount, total, reach, lean), jnp.int32)
    couples = (amount - 1) // 2
    source_of, sink = tallies[1:1 + 2 * couples:2], tallies[2:2 + 2 * couples:2]
    margin = jnp.minimum(source_of - 1, reach - sink)
    shifted = jax.random.randint(jax.random.fold_in(stream_key, 1), (couples,), 0, 1 << 20) % (margin + 1)
    tallies = tallies.at[1:1 + 2 * couples:2].set(source_of - shifted).at[2:2 + 2 * couples:2].set(sink + shifted)
    return tallies[jax.random.permutation(jax.random.fold_in(stream_key, 2), amount)]


def noise(own_key, extent, deviation, limit, cuts=(), kind=jnp.bfloat16):
    level = block_levels(own_key, extent, cuts, -0.22, 0.18) if cuts else 1.0
    entries = jax.random.normal(own_key, extent, jnp.float32) * deviation * level
    return jnp.minimum(jnp.maximum(entries, -limit), limit).astype(kind)


def setup_inputs(seed: int = 0) -> dict:
    key_of = jax.random.split(jax.random.key(seed), 7)
    return {
        "velocity": noise(key_of[0], (3, NX, NY, NZ), 1.0, 6.0, ((1, 8), (2, 16)), jnp.float32),
        "pressure": noise(key_of[1], (NX, NY, NZ), 2.0, 12.0, ((0, 8), (1, 16)), jnp.float32),
        "level_set": noise(key_of[2], (NX, NY, NZ), 2.0, 12.0, ((0, 8), (1, 16)), jnp.float32),
        "overset": draw_overset(jax.random.fold_in(key_of[6], 71), 0),
        "band_count": jax.vmap(lambda own: uneven_parts(own, N_COL, BAND_DEV * N_COL, MAXB, 2))(jax.random.split(key_of[4], N_BRICK)).reshape((N_BRICK, N_COL)).astype(jnp.int32),
        "band_ids": jax.vmap(lambda own: jax.random.permutation(own, BLK_DEV))(jax.random.split(key_of[5], N_BRICK * N_COL)).reshape((N_BRICK, N_COL, BLK_DEV)).astype(jnp.int32),
    }


DT = 0.1
VISC = 0.5
DT_SET = 0.2
TAU = 0.5

def predict(speed, plus, minus, p_plus, p_minus, overset):
    total = plus[0] + minus[0] + (plus[1] + minus[1]) + (plus[2] + minus[2])
    lapl = total - 6.0 * speed
    conv = speed[0:1] * (plus[0] - minus[0]) * 0.5 + speed[1:2] * (plus[1] - minus[1]) * 0.5 + speed[2:3] * (plus[2] - minus[2]) * 0.5
    grad = jnp.stack([(p_plus[d] - p_minus[d]) * 0.5 for d in range(3)])
    pred = speed + DT * (VISC * lapl - conv - grad)
    mean = total / 6.0
    kinds = overset[None]
    return jnp.where(kinds == 1, mean, jnp.where(kinds == 2, jnp.zeros_like(pred), pred))

def differences(field):
    inner = field[1:-1, 1:-1, 1:-1]
    back = [inner - field[:-2, 1:-1, 1:-1], inner - field[1:-1, :-2, 1:-1], inner - field[1:-1, 1:-1, :-2]]
    ahead = [field[2:, 1:-1, 1:-1] - inner, field[1:-1, 2:, 1:-1] - inner, field[1:-1, 1:-1, 2:] - inner]
    return (inner, back, ahead)

def band_update(cube):
    inner, back, ahead = differences(cube[0])
    speed = cube[1:4, 1:-1, 1:-1, 1:-1]
    flux = jnp.maximum(speed[0], 0.0) * back[0] + jnp.minimum(speed[0], 0.0) * ahead[0]
    flux = flux + (jnp.maximum(speed[1], 0.0) * back[1] + jnp.minimum(speed[1], 0.0) * ahead[1])
    flux = flux + (jnp.maximum(speed[2], 0.0) * back[2] + jnp.minimum(speed[2], 0.0) * ahead[2])
    psi = inner - DT_SET * flux
    sign_full = psi / jnp.sqrt(psi * psi + 1.0)
    size = psi.shape[0]
    for step in range(REINIT):
        inner, back, ahead = differences(psi)
        sgn = sign_full[step + 1:size - step - 1, step + 1:size - step - 1, step + 1:size - step - 1]
        gpos = jnp.zeros_like(inner)
        gneg = jnp.zeros_like(inner)
        for d in range(3):
            lower_p = jnp.maximum(back[d], 0.0)
            upper_p = jnp.minimum(ahead[d], 0.0)
            lower_n = jnp.minimum(back[d], 0.0)
            upper_n = jnp.maximum(ahead[d], 0.0)
            gpos = gpos + jnp.maximum(lower_p * lower_p, upper_p * upper_p)
            gneg = gneg + jnp.maximum(lower_n * lower_n, upper_n * upper_n)
        slope = jnp.sqrt(jnp.where(sgn > 0, gpos, gneg))
        psi = inner - TAU * sgn * (slope - 1.0)
    return psi.reshape(-1)

def to_blocks(field, nbx, nby, nbz):
    return field.reshape(nbx, BS, nby, BS, nbz, BS).transpose(0, 2, 4, 1, 3, 5).reshape(nbx * nby * nbz, BS ** 3)

def from_blocks(blocks, nbx, nby, nbz):
    return blocks.reshape(nbx, nby, nbz, BS, BS, BS).transpose(0, 3, 1, 4, 2, 5).reshape(nbx * BS, nby * BS, nbz * BS)

def reference(velocity, pressure, level_set, overset, band_count, band_ids):
    plus = [jnp.roll(velocity, -1, axis=d + 1) for d in range(3)]
    minus = [jnp.roll(velocity, 1, axis=d + 1) for d in range(3)]
    p_plus = [jnp.roll(pressure, -1, axis=d) for d in range(3)]
    p_minus = [jnp.roll(pressure, 1, axis=d) for d in range(3)]
    velocity_star = predict(velocity, plus, minus, p_plus, p_minus, overset)
    fields = jnp.concatenate([level_set[None], velocity], 0)
    padded = jnp.pad(fields, ((0, 0), (RIM, RIM), (RIM, RIM), (RIM, RIM)), mode='wrap')
    nbx_dev = CX // BS
    nby_dev = CY // BS
    nbz = CZ // BS
    gby = NY // BS
    total_blocks = NX // BS * gby * nbz
    zero = jnp.zeros((), jnp.int32)

    def per_device(dev):
        row = dev // N_COL
        column = dev % N_COL
        ids = band_ids[row, column, :MAXB].astype(jnp.int32)
        count = band_count[row, column]
        bx = ids // (nby_dev * nbz)
        by = ids // nbz % nby_dev
        bz = ids % nbz
        x0 = (row * CX + BS * bx).astype(jnp.int32)
        y0 = (column * CY + BS * by).astype(jnp.int32)
        z0 = (BS * bz).astype(jnp.int32)

        def one(xs, ys, zs):
            cube = lax.dynamic_slice(padded, (zero, xs, ys, zs), (4, CUBE, CUBE, CUBE))
            return band_update(cube)
        results = jax.vmap(one)(x0, y0, z0)
        live = jnp.arange(MAXB, dtype=jnp.int32) < count
        gidx = ((row * nbx_dev + bx) * gby + (column * nby_dev + by)) * nbz + bz
        gidx = jnp.where(live, gidx, total_blocks).astype(jnp.int32)
        return (results, gidx)
    results, gidx = lax.map(per_device, jnp.arange(N_BRICK * N_COL, dtype=jnp.int32))
    blocks = to_blocks(level_set, NX // BS, gby, nbz)
    blocks = blocks.at[gidx.reshape(-1)].set(results.reshape(-1, BS ** 3), mode='drop')
    level_set_new = from_blocks(blocks, NX // BS, gby, nbz)
    return (velocity_star, level_set_new)
```

```python
import functools

import jax
import jax.numpy as jnp
from jax import lax
from jax.experimental import pallas as pl
from jax.experimental.pallas import tpu as pltpu
from jax.sharding import PartitionSpec as P

BS = 16
REINIT = 3
MAXB = 16
RIM = 4
DEEP = 3
SLABS = RIM + 3 * DEEP + 1
CORNER = (DEEP * SLABS + 7) // 8 * 8
LEFT = 8

DT = 0.1
VISC = 0.5
DT_SET = 0.2
TAU = 0.5

ANY = pl.BlockSpec(memory_space=pl.ANY)
VM = pl.BlockSpec(memory_space=pltpu.VMEM)
SM = pl.BlockSpec(memory_space=pltpu.SMEM)


def run_all(copies):
    for copy in copies:
        copy.start()
    for copy in copies:
        copy.wait()


def pack_kernel(vel, press, level, x_lo, x_hi, y_lo, y_hi, sems):
    size_x, size_y = level.shape[:2]
    pairs = []
    for out, high in ((x_lo, False), (x_hi, True)):
        def rows(n):
            return pl.ds(size_x - n if high else 0, n)

        pairs.append((level.at[rows(RIM)], out.at[pl.ds(0, RIM)]))
        for i in range(3):
            pairs.append((vel.at[i, rows(DEEP)], out.at[pl.ds(RIM + i * DEEP, DEEP)]))
        pairs.append((press.at[rows(1)], out.at[pl.ds(RIM + 3 * DEEP, 1)]))
    for out, high in ((y_lo, False), (y_hi, True)):
        def cols(n):
            return pl.ds(size_y - n if high else 0, n)

        pairs.append((level.at[:, cols(RIM)], out.at[:, pl.ds(0, RIM)]))
        for i in range(3):
            pairs.append((vel.at[i, :, cols(DEEP)], out.at[:, pl.ds(RIM + i * DEEP, DEEP)]))
        pairs.append((press.at[:, cols(1)], out.at[:, pl.ds(RIM + 3 * DEEP, 1)]))
    run_all([pltpu.make_async_copy(s, d, sems.at[i]) for i, (s, d) in enumerate(pairs)])


def pack(velocity, pressure, level_set):
    size_x, size_y, size_z = level_set.shape
    f32 = jnp.float32
    return pl.pallas_call(
        pack_kernel,
        out_shape=[
            jax.ShapeDtypeStruct((SLABS, size_y, 1, size_z), f32),
            jax.ShapeDtypeStruct((SLABS, size_y, 1, size_z), f32),
            jax.ShapeDtypeStruct((size_x, SLABS, 1, size_z), f32),
            jax.ShapeDtypeStruct((size_x, SLABS, 1, size_z), f32),
        ],
        in_specs=[ANY] * 3,
        out_specs=[ANY] * 4,
        scratch_shapes=[pltpu.SemaphoreType.DMA((20,))],
        name="pack",
    )(
        velocity.reshape(3, size_x, size_y, 1, size_z),
        pressure.reshape(size_x, size_y, 1, size_z),
        level_set.reshape(size_x, size_y, 1, size_z),
    )


def relay_kernel(q_lo, q_hi, z_lo, z_hi, sems):
    rows = q_lo.shape[0]
    pairs = []
    for out, start in ((z_lo, 0), (z_hi, rows - CORNER)):
        for side, q in enumerate((q_lo, q_hi)):
            pairs.append((q.at[pl.ds(start, CORNER)], out.at[pl.ds(side * CORNER, CORNER)]))
    run_all([pltpu.make_async_copy(s, d, sems.at[i]) for i, (s, d) in enumerate(pairs)])


def relay(q_lo, q_hi):
    shape = jax.ShapeDtypeStruct((2 * CORNER,) + q_lo.shape[1:], jnp.float32)
    return pl.pallas_call(
        relay_kernel,
        out_shape=[shape, shape],
        in_specs=[ANY] * 2,
        out_specs=[ANY] * 2,
        scratch_shapes=[pltpu.SemaphoreType.DMA((4,))],
        name="relay",
    )(q_lo, q_hi)


def turn(value):
    return pltpu.roll(value, 1, 1), pltpu.roll(value, value.shape[1] - 1, 1)


def predict_kernel(vel, press, overset, x_lo, x_hi, q_lo, q_hi, out, V, R, K, O, X, Q, sems, osems):
    size_x, size_y = press.shape[:2]
    base = pl.program_id(0)
    body = pl.ds(LEFT, size_y)
    inner = pl.ds(1, size_x)
    pairs = [(vel.at[i], V.at[i, inner, body]) for i in range(3)]
    pairs += [(press, R.at[inner, body]), (overset, K)]
    for side, (x, place) in enumerate(((x_lo, 0), (x_hi, size_x + 1))):
        for i in range(3):
            near = RIM + i * DEEP + (0 if side else DEEP - 1)
            pairs.append((x.at[pl.ds(near, 1)], V.at[i, pl.ds(place, 1), body]))
        pairs.append((x.at[pl.ds(RIM + 3 * DEEP, 1)], R.at[pl.ds(place, 1), body]))
    pairs += [(q_lo, Q.at[0]), (q_hi, Q.at[1])]
    run_all([pltpu.make_async_copy(s, d, sems.at[i]) for i, (s, d) in enumerate(pairs)])

    def unpack(x, carry):
        for side, place in enumerate((LEFT - 1, LEFT + size_y)):
            for i in range(3):
                near = RIM + i * DEEP + (0 if side else DEEP - 1)
                V[i, x + 1, pl.ds(place, 1), :] = Q[side, pl.ds(x * SLABS + near, 1), :]
            R[x + 1, pl.ds(place, 1), :] = Q[side, pl.ds(x * SLABS + RIM + 3 * DEEP, 1), :]
        return carry

    lax.fori_loop(0, size_x, unpack, 0)

    def row(x, carry):
        for t in range(size_y // 8):
            y = LEFT + 8 * t

            def at(ref, dx, dy, *lead):
                start = y if dy == 0 else base + (y + dy)
                return ref[(*lead, x + (1 + dx), pl.ds(start, 8), slice(None))]

            kinds = K[x, pl.ds(8 * t, 8), :]
            rc = at(R, 0, 0)
            rm, rp = turn(rc)
            grads = (
                at(R, 1, 0) - at(R, -1, 0),
                at(R, 0, 1) - at(R, 0, -1),
                rp - rm,
            )
            speed = [at(V, 0, 0, i) for i in range(3)]
            for i in range(3):
                zm, zp = turn(speed[i])
                plus = (at(V, 1, 0, i), at(V, 0, 1, i), zp)
                minus = (at(V, -1, 0, i), at(V, 0, -1, i), zm)
                total = (plus[0] + minus[0]) + (plus[1] + minus[1]) + (plus[2] + minus[2])
                conv = (
                    speed[0] * (plus[0] - minus[0])
                    + speed[1] * (plus[1] - minus[1])
                    + speed[2] * (plus[2] - minus[2])
                )
                pred = speed[i] + DT * (
                    VISC * (total - 6.0 * speed[i]) - 0.5 * (conv + grads[i])
                )
                mean = total * (1.0 / 6.0)
                O[i, x, pl.ds(8 * t, 8), :] = jnp.where(
                    kinds == 1, mean, jnp.where(kinds == 2, 0.0, pred)
                )
        return carry

    chunks = 4
    step = size_x // chunks
    sent = []
    for c in range(chunks):
        lax.fori_loop(c * step, (c + 1) * step, row, 0)
        part = pl.ds(c * step, step)
        copy = pltpu.make_async_copy(O.at[:, part], out.at[:, part], osems.at[c])
        copy.start()
        sent.append(copy)
    for copy in sent:
        copy.wait()


def predictor(velocity, pressure, overset, x_lo, x_hi, q_lo, q_hi):
    size_x, size_y, size_z = pressure.shape
    f32 = jnp.float32
    wide = LEFT + size_y + 8
    return pl.pallas_call(
        predict_kernel,
        grid=(1,),
        out_shape=jax.ShapeDtypeStruct(velocity.shape, f32),
        in_specs=[ANY] * 7,
        out_specs=ANY,
        scratch_shapes=[
            pltpu.VMEM((3, size_x + 2, wide, size_z), f32),
            pltpu.VMEM((size_x + 2, wide, size_z), f32),
            pltpu.VMEM((size_x, size_y, size_z), jnp.int32),
            pltpu.VMEM((3, size_x, size_y, size_z), f32),
            pltpu.VMEM((8, size_z), f32),
            pltpu.VMEM((2, size_x * SLABS, size_z), f32),
            pltpu.SemaphoreType.DMA((15,)),
            pltpu.SemaphoreType.DMA((4,)),
        ],
        cost_estimate=pl.CostEstimate(
            flops=70 * 1024 * 128, bytes_accessed=5 << 20, transcendentals=0
        ),
        compiler_params=pltpu.CompilerParams(vmem_limit_bytes=24 << 20),
        name="predictor",
    )(velocity, pressure, overset, x_lo, x_hi, q_lo, q_hi)


def level_kernel(
    vel, level, x_lo, x_hi, q_lo, q_hi, z_lo, z_hi, count, ids, out,
    V, L, A, B, S, O, M, Q, Z, sems, osems,
):
    size_x, size_y, size_z = level.shape
    base = pl.program_id(0)
    body = pl.ds(LEFT, size_y)
    inner = pl.ds(RIM, size_x)
    pairs = [(level, L.at[inner, body])]
    pairs += [(vel.at[i], V.at[i, inner, body]) for i in range(3)]
    for x, far, close in ((x_lo, 0, RIM - DEEP), (x_hi, RIM + size_x, RIM + size_x)):
        pairs.append((x.at[pl.ds(0, RIM)], L.at[pl.ds(far, RIM), body]))
        for i in range(3):
            pairs.append(
                (x.at[pl.ds(RIM + i * DEEP, DEEP)], V.at[i, pl.ds(close, DEEP), body])
            )
    pairs += [(q_lo, Q.at[0]), (q_hi, Q.at[1]), (z_lo, Z.at[0]), (z_hi, Z.at[1])]
    copies = [pltpu.make_async_copy(s, d, sems.at[i]) for i, (s, d) in enumerate(pairs)]
    for copy in copies:
        copy.start()

    wide = size_y // BS
    deep = size_z // BS
    lane = lax.broadcasted_iota(jnp.int32, (8, size_z), 1) // BS
    marks = [jnp.zeros((8, size_z), jnp.bool_) for _ in range(size_x // BS * wide)]
    held = count[0]
    for s in range(MAXB):
        block = jnp.where(s < held, ids[s], -1)
        marks = [m | (lane == block - k * deep) for k, m in enumerate(marks)]
    for k, m in enumerate(marks):
        M[k] = m.astype(jnp.float32)

    for copy in copies:
        copy.wait()

    def fill(x, side, rows, ref, first):
        place = LEFT + size_y if side else LEFT - RIM
        L[x, pl.ds(place, RIM), :] = ref[(*rows, pl.ds(first, RIM), slice(None))]
        place = LEFT + size_y if side else LEFT - DEEP
        for i in range(3):
            V[i, x, pl.ds(place, DEEP), :] = ref[
                (*rows, pl.ds(first + RIM + i * DEEP, DEEP), slice(None))
            ]

    def unpack(x, carry):
        for side in range(2):
            fill(x + RIM, side, (side,), Q, x * SLABS)
        return carry

    lax.fori_loop(0, size_x, unpack, 0)
    skipped = CORNER - DEEP * SLABS
    for k in range(DEEP):
        for side in range(2):
            fill(RIM - DEEP + k, side, (0, side), Z, skipped + k * SLABS)
            fill(RIM + size_x + k, side, (1, side), Z, k * SLABS)

    tiles = (size_y + 2 * RIM) // 8

    def at(ref, x, y, *lead):
        return ref[(*lead, x, pl.ds(base + y, 8), slice(None))]

    def first_row(x, carry):
        for t in range(tiles):
            y = LEFT - RIM + 8 * t
            c = at(L, x, y)
            zm, zp = turn(c)
            v = [at(V, x, y, i) for i in range(3)]
            flux = jnp.maximum(v[0], 0.0) * (c - at(L, x - 1, y))
            flux += jnp.minimum(v[0], 0.0) * (at(L, x + 1, y) - c)
            flux += jnp.maximum(v[1], 0.0) * (c - at(L, x, y - 1))
            flux += jnp.minimum(v[1], 0.0) * (at(L, x, y + 1) - c)
            flux += jnp.maximum(v[2], 0.0) * (c - zm)
            flux += jnp.minimum(v[2], 0.0) * (zp - c)
            psi = c - DT_SET * flux
            A[x, pl.ds(base + y, 8), :] = psi
            S[x, pl.ds(base + y, 8), :] = (TAU * psi) * lax.rsqrt(psi * psi + 1.0)
        return carry

    lax.fori_loop(1, size_x + 2 * RIM - 1, first_row, 0)

    def evolve(ref, x, y):
        c = at(ref, x, y)
        s = at(S, x, y)
        zm, zp = turn(c)
        up = s > 0
        g = None
        for m, p in (
            (at(ref, x - 1, y), at(ref, x + 1, y)),
            (at(ref, x, y - 1), at(ref, x, y + 1)),
            (zm, zp),
        ):
            low = c - jnp.minimum(jnp.minimum(m, p), c)
            high = jnp.maximum(jnp.maximum(m, p), c) - c
            d = jnp.where(up, low, high)
            g = d * d if g is None else g + d * d
        return c - s * (jnp.sqrt(g) - 1.0)

    source, target = A, B
    for step in range(1, REINIT):
        def row(x, carry, source=source, target=target):
            for t in range(tiles):
                y = LEFT - RIM + 8 * t
                target[x, pl.ds(base + y, 8), :] = evolve(source, x, y)
            return carry

        lax.fori_loop(1 + step, size_x + 2 * RIM - 1 - step, row, 0)
        source, target = target, source

    def last_row(x, carry):
        for t in range(size_y // 8):
            y = LEFT + 8 * t
            mark = M[x // BS * wide + 8 * t // BS]
            new = evolve(source, x + RIM, y)
            old = L[x + RIM, pl.ds(y, 8), :]
            O[x, pl.ds(8 * t, 8), :] = jnp.where(mark > 0.5, new, old)
        return carry

    chunks = 4
    step = size_x // chunks
    sent = []
    for c in range(chunks):
        lax.fori_loop(c * step, (c + 1) * step, last_row, 0)
        part = pl.ds(c * step, step)
        copy = pltpu.make_async_copy(O.at[part], out.at[part], osems.at[c])
        copy.start()
        sent.append(copy)
    for copy in sent:
        copy.wait()


def level_update(velocity, level_set, x_lo, x_hi, q_lo, q_hi, z_lo, z_hi, count, ids):
    size_x, size_y, size_z = level_set.shape
    f32 = jnp.float32
    wide = LEFT + size_y + 8
    whole = (size_x + 2 * RIM, wide, size_z)
    return pl.pallas_call(
        level_kernel,
        grid=(1,),
        out_shape=jax.ShapeDtypeStruct(level_set.shape, f32),
        in_specs=[ANY] * 8 + [SM] * 2,
        out_specs=ANY,
        scratch_shapes=[
            pltpu.VMEM((3,) + whole, f32),
            pltpu.VMEM(whole, f32),
            pltpu.VMEM(whole, f32),
            pltpu.VMEM(whole, f32),
            pltpu.VMEM(whole, f32),
            pltpu.VMEM((size_x, size_y, size_z), f32),
            pltpu.VMEM((size_x // BS * (size_y // BS), 8, size_z), f32),
            pltpu.VMEM((2, size_x * SLABS, size_z), f32),
            pltpu.VMEM((2, 2, CORNER, size_z), f32),
            pltpu.SemaphoreType.DMA((16,)),
            pltpu.SemaphoreType.DMA((4,)),
        ],
        cost_estimate=pl.CostEstimate(
            flops=140 * 1600 * 128, bytes_accessed=4 << 20, transcendentals=0
        ),
        compiler_params=pltpu.CompilerParams(vmem_limit_bytes=24 << 20),
        name="level",
    )(velocity, level_set, x_lo, x_hi, q_lo, q_hi, z_lo, z_hi, count, ids)


def moved(array, axis, step):
    peers = lax.axis_size(axis)
    return lax.ppermute(array, axis, [(i, (i + step) % peers) for i in range(peers)])


def shards(velocity, pressure, level_set, overset, band_count, band_ids):
    size_x, size_y, size_z = level_set.shape
    x_low, x_high, y_low, y_high = pack(velocity, pressure, level_set)
    q_lo = moved(y_high, "col", 1)
    q_hi = moved(y_low, "col", -1)
    x_lo = moved(x_high, "brick", 1)
    x_hi = moved(x_low, "brick", -1)
    q_lo = q_lo.reshape(size_x * SLABS, 1, size_z)
    q_hi = q_hi.reshape(size_x * SLABS, 1, size_z)
    z_low, z_high = relay(q_lo, q_hi)
    z_lo = moved(z_high, "brick", 1)
    z_hi = moved(z_low, "brick", -1)
    x_lo = x_lo.reshape(SLABS, size_y, size_z)
    x_hi = x_hi.reshape(SLABS, size_y, size_z)
    q_lo = q_lo.reshape(size_x * SLABS, size_z)
    q_hi = q_hi.reshape(size_x * SLABS, size_z)
    z_lo = z_lo.reshape(2, CORNER, size_z)
    z_hi = z_hi.reshape(2, CORNER, size_z)
    velocity_star = predictor(velocity, pressure, overset, x_lo, x_hi, q_lo, q_hi)
    level_set_new = level_update(
        velocity, level_set, x_lo, x_hi, q_lo, q_hi, z_lo, z_hi,
        band_count.reshape(1), band_ids.reshape(-1),
    )
    return (velocity_star, level_set_new)


def solution(mesh):
    return jax.shard_map(
        shards,
        mesh=mesh,
        in_specs=(
            P(None, "brick", "col", None),
            P("brick", "col", None),
            P("brick", "col", None),
            P("brick", "col", None),
            P("brick", "col"),
            P("brick", "col", None),
        ),
        out_specs=(P(None, "brick", "col", None), P("brick", "col", None)),
        check_vma=False,
    )
```

```python
import functools

import jax
import jax.numpy as jnp
from jax import lax
from jax.experimental import pallas as pl
from jax.experimental.pallas import tpu as pltpu
from jax.sharding import PartitionSpec as P

BS = 16
REINIT = 3
MAXB = 16
RIM = 4
DEEP = 3
SLABS = RIM + 3 * DEEP + 1
CORNER = (DEEP * SLABS + 7) // 8 * 8
LEFT = 8
UNROLL = 52

DT = 0.1
VISC = 0.5
DT_SET = 0.2
TAU = 0.5

F32 = jnp.float32
ANY = pl.BlockSpec(memory_space=pl.ANY)
VM = pl.BlockSpec(memory_space=pltpu.VMEM)
SM = pl.BlockSpec(memory_space=pltpu.SMEM)


def call(kernel, args, outs, name, aliases=None, sems=0, flops=1 << 20):
    specs = {"vmem": VM, "hbm": ANY, "smem": SM}
    spaces = {"vmem": pltpu.VMEM, "hbm": pltpu.HBM}
    operands = [
        pltpu.with_memory_space_constraint(a, spaces[k]) if k in spaces else a for k, a in args
    ]
    shapes = [
        pltpu.VMEM(s, t) if k == "vmem" else jax.ShapeDtypeStruct(s, t) for k, s, t in outs
    ]
    return pl.pallas_call(
        kernel,
        out_shape=shapes,
        in_specs=[specs[k] for k, _ in args],
        out_specs=[specs[k] for k, _, _ in outs],
        input_output_aliases=aliases or {},
        scratch_shapes=[pltpu.SemaphoreType.DMA((sems,))] if sems else [],
        cost_estimate=pl.CostEstimate(
            flops=flops, bytes_accessed=4 << 20, transcendentals=0
        ),
        compiler_params=pltpu.CompilerParams(vmem_limit_bytes=8 << 20),
        name=name,
    )(*operands)


def copies_of(pairs, sems, first=0):
    return [
        pltpu.make_async_copy(s, d, sems.at[first + i]) for i, (s, d) in enumerate(pairs)
    ]


def start_all(copies):
    for copy in copies:
        copy.start()


def wait_all(copies):
    for copy in copies:
        copy.wait()


def sweep(low, high, tiles, cell):
    rows = high - low
    group = max(g for g in range(1, rows + 1) if rows % g == 0 and g * len(tiles) <= UNROLL)

    def some(i, carry):
        for k in range(group):
            for y in tiles:
                cell(low + i * group + k, y)
        return carry

    if group == rows:
        some(0, 0)
    else:
        lax.fori_loop(0, rows // group, some, 0)


def pack_kernel(vel, press, level, overset, x_lo, x_hi, y_lo, y_hi, V, L, R, K, sems):
    size_x, size_y = level.shape[:2]
    inner = pl.ds(RIM, size_x)
    fields = [(level, L)] + [(vel.at[i], V.at[i]) for i in range(3)] + [(press, R)]

    def part(first, count):
        return [
            (a.at[:, pl.ds(first, count)], b.at[inner, pl.ds(LEFT + first, count)])
            for a, b in fields
        ]

    edges = part(0, 8) + part(size_y - 8, 8)
    rest = []
    for out, high in ((x_lo, False), (x_hi, True)):
        def rows(n):
            return pl.ds(size_x - n if high else 0, n)

        rest.append((level.at[rows(RIM)], out.at[pl.ds(0, RIM)]))
        for i in range(3):
            rest.append((vel.at[i, rows(DEEP)], out.at[pl.ds(RIM + i * DEEP, DEEP)]))
        rest.append((press.at[rows(1)], out.at[pl.ds(RIM + 3 * DEEP, 1)]))
    rest += part(8, size_y - 16) + [(overset, K)]
    edges = copies_of(edges, sems)
    rest = copies_of(rest, sems, len(edges))
    start_all(edges + rest)
    wait_all(edges)

    def gather(x, y):
        for out, high in ((y_lo, False), (y_hi, True)):
            row = (x - RIM) * SLABS

            def take(ref, n, place, *lead):
                start = LEFT + (size_y - n if high else 0)
                out[pl.ds(row + place, n), :] = ref[(*lead, x, pl.ds(start, n), slice(None))]

            take(L, RIM, 0)
            for i in range(3):
                take(V, DEEP, RIM + i * DEEP, i)
            take(R, 1, RIM + 3 * DEEP)

    sweep(RIM, RIM + size_x, [0] * 6, lambda x, y: gather(x, y) if y == 0 else None)
    wait_all(rest)


def relay_kernel(after, q_lo, q_hi, z_lo, z_hi, sems):
    rows = q_lo.shape[0]
    pairs = []
    for out, start in ((z_lo, 0), (z_hi, rows - CORNER)):
        for side, q in enumerate((q_lo, q_hi)):
            pairs.append((q.at[pl.ds(start, CORNER)], out.at[side]))
    copies = copies_of(pairs, sems)
    start_all(copies)
    wait_all(copies)


def turn(value):
    return pltpu.roll(value, 1, 1), pltpu.roll(value, value.shape[1] - 1, 1)


def tile(ref, x, y, *lead):
    return ref[(*lead, x, pl.ds(y, 8), slice(None))]


def predict(V, R, K, VS, x, y):
    kinds = tile(K, x - RIM, y - LEFT)
    rm, rp = turn(tile(R, x, y))
    grads = (
        tile(R, x + 1, y) - tile(R, x - 1, y),
        tile(R, x, y + 1) - tile(R, x, y - 1),
        rp - rm,
    )
    speed = [tile(V, x, y, i) for i in range(3)]
    for i in range(3):
        zm, zp = turn(speed[i])
        plus = (tile(V, x + 1, y, i), tile(V, x, y + 1, i), zp)
        minus = (tile(V, x - 1, y, i), tile(V, x, y - 1, i), zm)
        total = (plus[0] + minus[0]) + (plus[1] + minus[1]) + (plus[2] + minus[2])
        conv = (
            speed[0] * (plus[0] - minus[0])
            + speed[1] * (plus[1] - minus[1])
            + speed[2] * (plus[2] - minus[2])
        )
        pred = speed[i] + DT * (VISC * (total - 6.0 * speed[i]) - 0.5 * (conv + grads[i]))
        mean = total * (1.0 / 6.0)
        VS[i, x - RIM, pl.ds(y - LEFT, 8), :] = jnp.where(
            kinds == 1, mean, jnp.where(kinds == 2, 0.0, pred)
        )


def advect(L, V, A, S, x, y):
    c = tile(L, x, y)
    zm, zp = turn(c)
    v = [tile(V, x, y, i) for i in range(3)]
    flux = jnp.maximum(v[0], 0.0) * (c - tile(L, x - 1, y))
    flux += jnp.minimum(v[0], 0.0) * (tile(L, x + 1, y) - c)
    flux += jnp.maximum(v[1], 0.0) * (c - tile(L, x, y - 1))
    flux += jnp.minimum(v[1], 0.0) * (tile(L, x, y + 1) - c)
    flux += jnp.maximum(v[2], 0.0) * (c - zm)
    flux += jnp.minimum(v[2], 0.0) * (zp - c)
    psi = c - DT_SET * flux
    A[x, pl.ds(y, 8), :] = psi
    S[x, pl.ds(y, 8), :] = (TAU * psi) * lax.rsqrt(psi * psi + 1.0)


def evolved(ref, S, x, y):
    c = tile(ref, x, y)
    s = tile(S, x, y)
    zm, zp = turn(c)
    up = s > 0
    g = None
    for m, p in (
        (tile(ref, x - 1, y), tile(ref, x + 1, y)),
        (tile(ref, x, y - 1), tile(ref, x, y + 1)),
        (zm, zp),
    ):
        low = c - jnp.minimum(jnp.minimum(m, p), c)
        high = jnp.maximum(jnp.maximum(m, p), c) - c
        d = jnp.where(up, low, high)
        g = d * d if g is None else g + d * d
    return c - s * (jnp.sqrt(g) - 1.0)


def evolve(source, target, S, x, y):
    target[x, pl.ds(y, 8), :] = evolved(source, S, x, y)


def finish(source, S, L, M, F, size_y, x, y):
    new = evolved(source, S, x, y)
    y0 = max(y, LEFT)
    y1 = min(y + 8, LEFT + size_y)
    wide = size_y // BS
    first = (y0 - LEFT) // BS
    last = (y1 - 1 - LEFT) // BS
    mark = M[(x - RIM) // BS * wide + first]
    if first != last:
        edge = LEFT + last * BS - y
        rows = lax.broadcasted_iota(jnp.int32, mark.shape, 0)
        mark = jnp.where(rows < edge, mark, M[(x - RIM) // BS * wide + last])
    value = jnp.where(mark > 0.5, new, tile(L, x, y))
    F[x - RIM, pl.ds(y0 - LEFT, y1 - y0), :] = value[y0 - y : y1 - y]


def inner_kernel(V, L, R, K, count, ids, VS, A, S, B, C, F, M):
    size_x, size_y, size_z = F.shape
    wide = size_y // BS
    deep = size_z // BS
    lane = lax.broadcasted_iota(jnp.int32, (8, size_z), 1) // BS
    marks = [jnp.zeros((8, size_z), jnp.bool_) for _ in range(size_x // BS * wide)]
    held = count[0, 0]
    for s in range(MAXB):
        block = jnp.where(s < held, ids[0, 0, s], -1)
        marks = [m | (lane == block - k * deep) for k, m in enumerate(marks)]
    for k, m in enumerate(marks):
        M[k] = m.astype(F32)

    core = [LEFT + y for y in range(0, size_y, 8)]
    mid = [LEFT + y for y in range(RIM, size_y - RIM, 8)]
    low, high = RIM, RIM + size_x
    sweep(low + 1, high - 1, core, functools.partial(advect, L, V, A, S))
    sweep(low + 2, high - 2, core, functools.partial(evolve, A, B, S))
    sweep(low + 3, high - 3, core, functools.partial(evolve, B, C, S))
    sweep(low + 4, high - 4, mid, functools.partial(finish, C, S, L, M, F, size_y))
    sweep(low + 1, high - 1, core[1:-1], functools.partial(predict, V, R, K, VS))


def edge_kernel(
    K, M, x_lo, x_hi, q_lo, q_hi, *refs
):
    V, L, R, VS, A, S, B, C, F, star, sems = refs[9:]
    size_x, size_y = F.shape[:2]
    body = pl.ds(LEFT, size_y)
    low, high = RIM, RIM + size_x
    pairs = []
    for side, x in enumerate((x_lo, x_hi)):
        place = high if side else low - RIM
        pairs.append((x.at[pl.ds(0, RIM)], L.at[pl.ds(place, RIM), body]))
        place = high if side else low - DEEP
        for i in range(3):
            pairs.append(
                (x.at[pl.ds(RIM + i * DEEP, DEEP)], V.at[i, pl.ds(place, DEEP), body])
            )
        place = high if side else low - 1
        pairs.append((x.at[pl.ds(RIM + 3 * DEEP, 1)], R.at[pl.ds(place, 1), body]))
    copies = copies_of(pairs, sems)
    start_all(copies)

    def spread(x, y):
        for side, q in enumerate((q_lo, q_hi)):
            fill(L, V, x, side, q, (), (x - RIM) * SLABS, size_y)
            place = LEFT + size_y if side else LEFT - 1
            R[x, pl.ds(place, 1), :] = q[pl.ds((x - RIM) * SLABS + RIM + 3 * DEEP, 1), :]

    sweep(low, high, [0] * 6, lambda x, y: spread(x, y) if y == 0 else None)
    wait_all(copies)

    core = [LEFT + y for y in range(0, size_y, 8)]
    mid = [LEFT + y for y in range(RIM, size_y - RIM, 8)]
    outer = [LEFT - RIM, LEFT + size_y - RIM]
    step = functools.partial(predict, V, R, K, VS)
    sweep(low + 1, high - 1, [core[0], core[-1]], step)
    for x in (low, high - 1):
        for y in core:
            step(x, y)
    out = copies_of([(VS.at[i], star.at[i]) for i in range(3)], sems, len(copies))
    start_all(out)

    def ring(depth, cell):
        sweep(low - depth, high + depth, outer, cell)
        sweep(low - depth, low - depth + 4, mid, cell)
        sweep(high + depth - 4, high + depth, mid, cell)

    ring(3, functools.partial(advect, L, V, A, S))
    ring(2, functools.partial(evolve, A, B, S))
    ring(1, functools.partial(evolve, B, C, S))
    ring(0, functools.partial(finish, C, S, L, M, F, size_y))
    wait_all(out)


def fill(L, V, x, side, ref, lead, first, size_y):
    place = LEFT + size_y if side else LEFT - RIM
    L[x, pl.ds(place, RIM), :] = ref[(*lead, pl.ds(first, RIM), slice(None))]
    place = LEFT + size_y if side else LEFT - DEEP
    for i in range(3):
        V[i, x, pl.ds(place, DEEP), :] = ref[
            (*lead, pl.ds(first + RIM + i * DEEP, DEEP), slice(None))
        ]


def corner_kernel(M, z_lo, z_hi, *refs):
    V, L, A, S, B, C, F, new, sems = refs[7:]
    size_x, size_y = F.shape[:2]
    low, high = RIM, RIM + size_x
    early = copies_of(
        [(F.at[pl.ds(3, size_x - 6)], new.at[pl.ds(3, size_x - 6)])], sems
    )
    start_all(early)
    skipped = CORNER - DEEP * SLABS
    for k in range(DEEP):
        for side in range(2):
            fill(L, V, low - DEEP + k, side, z_lo, (side,), skipped + k * SLABS, size_y)
            fill(L, V, high + k, side, z_hi, (side,), k * SLABS, size_y)

    outer = [LEFT - RIM, LEFT + size_y - RIM]

    def ends(depth, cell):
        rows = 4 if depth else 3
        for k in range(rows):
            for x in (low - depth + k, high + depth - 1 - k):
                for y in outer:
                    cell(x, y)

    ends(3, functools.partial(advect, L, V, A, S))
    ends(2, functools.partial(evolve, A, B, S))
    ends(1, functools.partial(evolve, B, C, S))
    ends(0, functools.partial(finish, C, S, L, M, F, size_y))
    late = copies_of(
        [(F.at[pl.ds(x, 3)], new.at[pl.ds(x, 3)]) for x in (0, size_x - 3)], sems, 1
    )
    start_all(late)
    wait_all(early + late)


def moved(array, axis, step):
    peers = lax.axis_size(axis)
    return lax.ppermute(array, axis, [(i, (i + step) % peers) for i in range(peers)])


def shards(velocity, pressure, level_set, overset, band_count, band_ids):
    size_x, size_y, size_z = level_set.shape
    plain = level_set.shape
    padded = (size_x + 2 * RIM, LEFT + size_y + 8, size_z)
    x_face = (SLABS, size_y, size_z)
    y_face = (size_x * SLABS, size_z)
    marks = (size_x // BS * (size_y // BS), 8, size_z)

    x_low, x_high, y_low, y_high, V, L, R, K = call(
        pack_kernel,
        [("hbm", velocity), ("hbm", pressure), ("hbm", level_set), ("hbm", overset)],
        [("vmem", x_face, F32)] * 2
        + [("vmem", y_face, F32)] * 2
        + [("vmem", (3,) + padded, F32), ("vmem", padded, F32), ("vmem", padded, F32)]
        + [("vmem", plain, jnp.int32)],
        "pack",
        sems=26,
    )
    q_lo = moved(y_high, "col", 1)
    q_hi = moved(y_low, "col", -1)
    x_lo = moved(x_high, "brick", 1)
    x_hi = moved(x_low, "brick", -1)
    VS, A, S, B, C, F, M = call(
        inner_kernel,
        [("vmem", V), ("vmem", L), ("vmem", R), ("vmem", K)]
        + [("smem", band_count), ("smem", band_ids)],
        [("vmem", (3,) + plain, F32)]
        + [("vmem", padded, F32)] * 4
        + [("vmem", plain, F32), ("vmem", marks, F32)],
        "inner",
        flops=60 << 20,
    )
    z_low, z_high = call(
        relay_kernel,
        [("vmem", M), ("vmem", q_lo), ("vmem", q_hi)],
        [("vmem", (2, CORNER, size_z), F32)] * 2,
        "relay",
        sems=4,
    )
    z_lo = moved(z_high, "brick", 1)
    z_hi = moved(z_low, "brick", -1)
    state = [V, L, R, VS, A, S, B, C, F]
    held = [("vmem", K), ("vmem", M)] + [("vmem", a) for a in (x_lo, x_hi, q_lo, q_hi)]
    *state, velocity_star = call(
        edge_kernel,
        held + [("vmem", a) for a in state],
        [("vmem", a.shape, F32) for a in state] + [("hbm", velocity.shape, F32)],
        "edge",
        aliases={len(held) + i: i for i in range(len(state))},
        sems=13,
        flops=60 << 20,
    )
    V, L, R, VS, A, S, B, C, F = state
    state = [V, L, A, S, B, C, F]
    held = [("vmem", M), ("vmem", z_lo), ("vmem", z_hi)]
    *state, level_set_new = call(
        corner_kernel,
        held + [("vmem", a) for a in state],
        [("vmem", a.shape, F32) for a in state] + [("hbm", plain, F32)],
        "corner",
        aliases={len(held) + i: i for i in range(len(state))},
        sems=3,
    )
    return (velocity_star, level_set_new)


def solution(mesh):
    return jax.shard_map(
        shards,
        mesh=mesh,
        in_specs=(
            P(None, "brick", "col", None),
            P("brick", "col", None),
            P("brick", "col", None),
            P("brick", "col", None),
            P("brick", "col"),
            P("brick", "col", None),
        ),
        out_specs=(P(None, "brick", "col", None), P("brick", "col", None)),
        check_vma=False,
    )
```

```python
import functools

import jax
import jax.numpy as jnp
from jax import lax
from jax.experimental import pallas as pl
from jax.experimental.pallas import tpu as pltpu
from jax.sharding import PartitionSpec as P

BS = 16
REINIT = 3
MAXB = 16
RIM = 4
DEEP = 3
SLABS = RIM + 3 * DEEP + 1
CORNER = (DEEP * SLABS + 7) // 8 * 8
LEFT = 8
UNROLL = 80

DT = 0.1
VISC = 0.5
DT_SET = 0.2
TAU = 0.5

F32 = jnp.float32
ANY = pl.BlockSpec(memory_space=pl.ANY)
VM = pl.BlockSpec(memory_space=pltpu.VMEM)
SM = pl.BlockSpec(memory_space=pltpu.SMEM)


def call(kernel, args, outs, name, aliases=None, sems=0, flops=1 << 20, scratch=()):
    specs = {"vmem": VM, "hbm": ANY, "smem": SM}
    spaces = {"vmem": pltpu.VMEM, "hbm": pltpu.HBM}
    operands = [
        pltpu.with_memory_space_constraint(a, spaces[k]) if k in spaces else a for k, a in args
    ]
    shapes = [
        pltpu.VMEM(s, t) if k == "vmem" else jax.ShapeDtypeStruct(s, t) for k, s, t in outs
    ]
    return pl.pallas_call(
        kernel,
        out_shape=shapes,
        in_specs=[specs[k] for k, _ in args],
        out_specs=[specs[k] for k, _, _ in outs],
        input_output_aliases=aliases or {},
        scratch_shapes=list(scratch) + [pltpu.SemaphoreType.DMA((sems,))],
        cost_estimate=pl.CostEstimate(
            flops=flops, bytes_accessed=4 << 20, transcendentals=0
        ),
        compiler_params=pltpu.CompilerParams(vmem_limit_bytes=8 << 20),
        name=name,
    )(*operands)


def copies_of(pairs, sems, first=0):
    return [
        pltpu.make_async_copy(s, d, sems.at[first + i]) for i, (s, d) in enumerate(pairs)
    ]


def start_all(copies):
    for copy in copies:
        copy.start()


def wait_all(copies):
    for copy in copies:
        copy.wait()


def sweep(low, high, tiles, cell):
    rows = high - low
    group = max(g for g in range(1, rows + 1) if rows % g == 0 and g * len(tiles) <= UNROLL)

    def some(i, carry):
        for k in range(group):
            for y in tiles:
                cell(low + i * group + k, y)
        return carry

    if group == rows:
        some(0, 0)
    else:
        lax.fori_loop(0, rows // group, some, 0)


def pack_kernel(vel, press, level, x_lo, x_hi, y_lo, y_hi, V, L, R, sems):
    size_x, size_y = level.shape[:2]
    inner = pl.ds(RIM, size_x)
    body = pl.ds(LEFT, size_y)
    fields = [(level, L)] + [(vel.at[i], V.at[i]) for i in range(3)] + [(press, R)]

    def part(first, count, fields):
        return [
            (a.at[:, pl.ds(first, count)], b.at[inner, pl.ds(LEFT + first, count)])
            for a, b in fields
        ]

    edges = part(0, 8, fields) + part(size_y - 8, 8, fields)
    rest = part(8, size_y - 16, fields[:-1])
    local = []
    for out, high in ((x_lo, False), (x_hi, True)):
        def rows(n, first=RIM):
            return pl.ds(first + (size_x - n if high else 0), n)

        local.append((L.at[rows(RIM), body], out.at[pl.ds(0, RIM)]))
        for i in range(3):
            local.append((V.at[i, rows(DEEP), body], out.at[pl.ds(RIM + i * DEEP, DEEP)]))
        rest.append((press.at[rows(1, 0)], out.at[pl.ds(RIM + 3 * DEEP, 1)]))
    edges = copies_of(edges, sems)
    rest = copies_of(rest, sems, len(edges))
    local = copies_of(local, sems, len(edges) + len(rest))
    start_all(edges + rest)
    wait_all(edges)

    def gather(x, y):
        for out, high in ((y_lo, False), (y_hi, True)):
            row = (x - RIM) * SLABS

            def take(ref, n, place, *lead):
                start = LEFT + (size_y - n if high else 0)
                out[pl.ds(row + place, n), :] = ref[(*lead, x, pl.ds(start, n), slice(None))]

            take(L, RIM, 0)
            for i in range(3):
                take(V, DEEP, RIM + i * DEEP, i)
            take(R, 1, RIM + 3 * DEEP)

    sweep(RIM, RIM + size_x, [0] * 6, lambda x, y: gather(x, y) if y == 0 else None)
    wait_all(rest)
    start_all(local)
    wait_all(local)


def relay_kernel(after, q_lo, q_hi, z_lo, z_hi, sems):
    rows = q_lo.shape[0]
    pairs = []
    for out, start in ((z_lo, 0), (z_hi, rows - CORNER)):
        for side, q in enumerate((q_lo, q_hi)):
            pairs.append((q.at[pl.ds(start, CORNER)], out.at[side]))
    copies = copies_of(pairs, sems)
    start_all(copies)
    wait_all(copies)


def turn(value):
    return pltpu.roll(value, 1, 1), pltpu.roll(value, value.shape[1] - 1, 1)


def tile(ref, x, y, *lead):
    return ref[(*lead, x, pl.ds(y, 8), slice(None))]


def predict(V, R, K, VS, x, y):
    kinds = tile(K, x - RIM, y - LEFT)
    rm, rp = turn(tile(R, x, y))
    grads = (
        tile(R, x + 1, y) - tile(R, x - 1, y),
        tile(R, x, y + 1) - tile(R, x, y - 1),
        rp - rm,
    )
    speed = [tile(V, x, y, i) for i in range(3)]
    for i in range(3):
        zm, zp = turn(speed[i])
        plus = (tile(V, x + 1, y, i), tile(V, x, y + 1, i), zp)
        minus = (tile(V, x - 1, y, i), tile(V, x, y - 1, i), zm)
        total = (plus[0] + minus[0]) + (plus[1] + minus[1]) + (plus[2] + minus[2])
        conv = (
            speed[0] * (plus[0] - minus[0])
            + speed[1] * (plus[1] - minus[1])
            + speed[2] * (plus[2] - minus[2])
        )
        pred = (1.0 - 6.0 * DT * VISC) * speed[i] + (
            DT * VISC * total - 0.5 * DT * (conv + grads[i])
        )
        mean = total * (1.0 / 6.0)
        VS[i, x - RIM, pl.ds(y - LEFT, 8), :] = jnp.where(
            kinds == 1, mean, jnp.where(kinds == 2, 0.0, pred)
        )


def advect(L, V, A, S, x, y):
    c = tile(L, x, y)
    zm, zp = turn(c)
    v = [tile(V, x, y, i) for i in range(3)]
    flux = None
    for u, m, p in (
        (v[0], tile(L, x - 1, y), tile(L, x + 1, y)),
        (v[1], tile(L, x, y - 1), tile(L, x, y + 1)),
        (v[2], zm, zp),
    ):
        term = u * jnp.where(u > 0, c - m, p - c)
        flux = term if flux is None else flux + term
    psi = c - DT_SET * flux
    A[x, pl.ds(y, 8), :] = psi
    S[x, pl.ds(y, 8), :] = (TAU * psi) * lax.rsqrt(psi * psi + 1.0)


def evolved(ref, S, x, y):
    c = tile(ref, x, y)
    s = tile(S, x, y)
    zm, zp = turn(c)
    up = s > 0
    g = None
    for m, p in (
        (tile(ref, x - 1, y), tile(ref, x + 1, y)),
        (tile(ref, x, y - 1), tile(ref, x, y + 1)),
        (zm, zp),
    ):
        low = c - jnp.minimum(jnp.minimum(m, p), c)
        high = jnp.maximum(jnp.maximum(m, p), c) - c
        d = jnp.where(up, low, high)
        g = d * d if g is None else g + d * d
    return c - s * (g * lax.rsqrt(g + 1e-30) - 1.0)


def evolve(source, target, S, x, y):
    target[x, pl.ds(y, 8), :] = evolved(source, S, x, y)


def finish(source, S, L, M, F, size_y, x, y):
    new = evolved(source, S, x, y)
    y0 = max(y, LEFT)
    y1 = min(y + 8, LEFT + size_y)
    wide = size_y // BS
    first = (y0 - LEFT) // BS
    last = (y1 - 1 - LEFT) // BS
    mark = M[(x - RIM) // BS * wide + first]
    if first != last:
        edge = LEFT + last * BS - y
        rows = lax.broadcasted_iota(jnp.int32, mark.shape, 0)
        mark = jnp.where(rows < edge, mark, M[(x - RIM) // BS * wide + last])
    value = jnp.where(mark > 0.5, new, tile(L, x, y))
    F[x - RIM, pl.ds(y0 - LEFT, y1 - y0), :] = value[y0 - y : y1 - y]


def inner_kernel(
    V, L, press, overset, count, band_ids, _, R, K, VS, A, S, B, C, F, M, ids, sems
):
    size_x, size_y, size_z = F.shape
    middle = size_y - 16
    named = copies_of([(band_ids, ids)], sems)
    later = copies_of(
        [
            (press.at[:, pl.ds(8, middle)], R.at[pl.ds(RIM, size_x), pl.ds(LEFT + 8, middle)]),
            (overset, K),
        ],
        sems,
        1,
    )
    start_all(named + later)
    core = [LEFT + y for y in range(0, size_y, 8)]
    mid = [LEFT + y for y in range(RIM, size_y - RIM, 8)]
    low, high = RIM, RIM + size_x
    sweep(low + 1, high - 1, core, functools.partial(advect, L, V, A, S))
    sweep(low + 2, high - 2, core, functools.partial(evolve, A, B, S))
    sweep(low + 3, high - 3, core, functools.partial(evolve, B, C, S))

    wait_all(named)
    wide = size_y // BS
    deep = size_z // BS
    lane = lax.broadcasted_iota(jnp.int32, (8, size_z), 1) // BS
    marks = [jnp.zeros((8, size_z), jnp.bool_) for _ in range(size_x // BS * wide)]
    held = count[0, 0]
    for s in range(MAXB):
        block = jnp.where(s < held, ids[0, 0, s], -1)
        marks = [m | (lane == block - k * deep) for k, m in enumerate(marks)]
    for k, m in enumerate(marks):
        M[k] = m.astype(F32)

    sweep(low + 4, high - 4, mid, functools.partial(finish, C, S, L, M, F, size_y))
    wait_all(later)
    sweep(low + 1, high - 1, core[1:-1], functools.partial(predict, V, R, K, VS))


def edge_kernel(
    K, M, x_lo, x_hi, q_lo, q_hi, *refs
):
    V, L, R, VS, A, S, B, C, F, star, sems = refs[9:]
    size_x, size_y = F.shape[:2]
    body = pl.ds(LEFT, size_y)
    low, high = RIM, RIM + size_x
    pairs = []
    for side, x in enumerate((x_lo, x_hi)):
        place = high if side else low - RIM
        pairs.append((x.at[pl.ds(0, RIM)], L.at[pl.ds(place, RIM), body]))
        place = high if side else low - DEEP
        for i in range(3):
            pairs.append(
                (x.at[pl.ds(RIM + i * DEEP, DEEP)], V.at[i, pl.ds(place, DEEP), body])
            )
        place = high if side else low - 1
        pairs.append((x.at[pl.ds(RIM + 3 * DEEP, 1)], R.at[pl.ds(place, 1), body]))
    copies = copies_of(pairs, sems)
    start_all(copies)

    def spread(x, y):
        for side, q in enumerate((q_lo, q_hi)):
            fill(L, V, x, side, q, (), (x - RIM) * SLABS, size_y)
            place = LEFT + size_y if side else LEFT - 1
            R[x, pl.ds(place, 1), :] = q[pl.ds((x - RIM) * SLABS + RIM + 3 * DEEP, 1), :]

    sweep(low, high, [0] * 6, lambda x, y: spread(x, y) if y == 0 else None)
    wait_all(copies)

    core = [LEFT + y for y in range(0, size_y, 8)]
    mid = [LEFT + y for y in range(RIM, size_y - RIM, 8)]
    outer = [LEFT - RIM, LEFT + size_y - RIM]
    step = functools.partial(predict, V, R, K, VS)
    sweep(low + 1, high - 1, [core[0], core[-1]], step)
    for x in (low, high - 1):
        for y in core:
            step(x, y)
    out = copies_of([(VS.at[i], star.at[i]) for i in range(3)], sems, len(copies))
    start_all(out)

    def ring(depth, cell):
        sweep(low - depth, high + depth, outer, cell)
        sweep(low - depth, low - depth + 4, mid, cell)
        sweep(high + depth - 4, high + depth, mid, cell)

    ring(3, functools.partial(advect, L, V, A, S))
    ring(2, functools.partial(evolve, A, B, S))
    ring(1, functools.partial(evolve, B, C, S))
    ring(0, functools.partial(finish, C, S, L, M, F, size_y))
    wait_all(out)


def fill(L, V, x, side, ref, lead, first, size_y):
    place = LEFT + size_y if side else LEFT - RIM
    L[x, pl.ds(place, RIM), :] = ref[(*lead, pl.ds(first, RIM), slice(None))]
    place = LEFT + size_y if side else LEFT - DEEP
    for i in range(3):
        V[i, x, pl.ds(place, DEEP), :] = ref[
            (*lead, pl.ds(first + RIM + i * DEEP, DEEP), slice(None))
        ]


def corner_kernel(M, z_lo, z_hi, *refs):
    V, L, A, S, B, C, F, new, sems = refs[7:]
    size_x, size_y = F.shape[:2]
    low, high = RIM, RIM + size_x
    early = copies_of(
        [(F.at[pl.ds(3, size_x - 6)], new.at[pl.ds(3, size_x - 6)])], sems
    )
    start_all(early)
    skipped = CORNER - DEEP * SLABS
    for k in range(DEEP):
        for side in range(2):
            fill(L, V, low - DEEP + k, side, z_lo, (side,), skipped + k * SLABS, size_y)
            fill(L, V, high + k, side, z_hi, (side,), k * SLABS, size_y)

    outer = [LEFT - RIM, LEFT + size_y - RIM]

    def ends(depth, cell):
        rows = 4 if depth else 3
        for k in range(rows):
            for x in (low - depth + k, high + depth - 1 - k):
                for y in outer:
                    cell(x, y)

    ends(3, functools.partial(advect, L, V, A, S))
    ends(2, functools.partial(evolve, A, B, S))
    ends(1, functools.partial(evolve, B, C, S))
    ends(0, functools.partial(finish, C, S, L, M, F, size_y))
    late = copies_of(
        [(F.at[pl.ds(x, 3)], new.at[pl.ds(x, 3)]) for x in (0, size_x - 3)], sems, 1
    )
    start_all(late)
    wait_all(early + late)


def moved(array, axis, step):
    peers = lax.axis_size(axis)
    return lax.ppermute(array, axis, [(i, (i + step) % peers) for i in range(peers)])


def shards(velocity, pressure, level_set, overset, band_count, band_ids):
    size_x, size_y, size_z = level_set.shape
    plain = level_set.shape
    padded = (size_x + 2 * RIM, LEFT + size_y + 8, size_z)
    x_face = (SLABS, size_y, size_z)
    y_face = (size_x * SLABS, size_z)
    marks = (size_x // BS * (size_y // BS), 8, size_z)

    x_low, x_high, y_low, y_high, V, L, R = call(
        pack_kernel,
        [("hbm", velocity), ("hbm", pressure), ("hbm", level_set)],
        [("vmem", x_face, F32)] * 2
        + [("vmem", y_face, F32)] * 2
        + [("vmem", (3,) + padded, F32), ("vmem", padded, F32), ("vmem", padded, F32)],
        "pack",
        sems=24,
    )
    q_lo = moved(y_high, "col", 1)
    q_hi = moved(y_low, "col", -1)
    x_lo = moved(x_high, "brick", 1)
    x_hi = moved(x_low, "brick", -1)
    R, K, VS, A, S, B, C, F, M = call(
        inner_kernel,
        [("vmem", V), ("vmem", L), ("hbm", pressure), ("hbm", overset)]
        + [("smem", band_count), ("hbm", band_ids), ("vmem", R)],
        [("vmem", padded, F32), ("vmem", plain, jnp.int32), ("vmem", (3,) + plain, F32)]
        + [("vmem", padded, F32)] * 4
        + [("vmem", plain, F32), ("vmem", marks, F32)],
        "inner",
        aliases={6: 0},
        scratch=[pltpu.SMEM(band_ids.shape, jnp.int32)],
        sems=3,
        flops=60 << 20,
    )
    z_low, z_high = call(
        relay_kernel,
        [("vmem", M), ("vmem", q_lo), ("vmem", q_hi)],
        [("vmem", (2, CORNER, size_z), F32)] * 2,
        "relay",
        sems=4,
    )
    z_lo = moved(z_high, "brick", 1)
    z_hi = moved(z_low, "brick", -1)
    state = [V, L, R, VS, A, S, B, C, F]
    held = [("vmem", K), ("vmem", M)] + [("vmem", a) for a in (x_lo, x_hi, q_lo, q_hi)]
    *state, velocity_star = call(
        edge_kernel,
        held + [("vmem", a) for a in state],
        [("vmem", a.shape, F32) for a in state] + [("hbm", velocity.shape, F32)],
        "edge",
        aliases={len(held) + i: i for i in range(len(state))},
        sems=13,
        flops=60 << 20,
    )
    V, L, R, VS, A, S, B, C, F = state
    state = [V, L, A, S, B, C, F]
    held = [("vmem", M), ("vmem", z_lo), ("vmem", z_hi)]
    *state, level_set_new = call(
        corner_kernel,
        held + [("vmem", a) for a in state],
        [("vmem", a.shape, F32) for a in state] + [("hbm", plain, F32)],
        "corner",
        aliases={len(held) + i: i for i in range(len(state))},
        sems=3,
    )
    return (velocity_star, level_set_new)


def solution(mesh):
    return jax.shard_map(
        shards,
        mesh=mesh,
        in_specs=(
            P(None, "brick", "col", None),
            P("brick", "col", None),
            P("brick", "col", None),
            P("brick", "col", None),
            P("brick", "col"),
            P("brick", "col", None),
        ),
        out_specs=(P(None, "brick", "col", None), P("brick", "col", None)),
        check_vma=False,
    )
```

```python
import functools

import jax
import jax.numpy as jnp
from jax import lax
from jax.experimental import pallas as pl
from jax.experimental.pallas import tpu as pltpu
from jax.sharding import PartitionSpec as P

BS = 16
REINIT = 3
MAXB = 16
RIM = 4
DEEP = 3
SLABS = RIM + 3 * DEEP + 1
CORNER = (DEEP * SLABS + 7) // 8 * 8
LEFT = 8
UNROLL = 80

DT = 0.1
VISC = 0.5
DT_SET = 0.2
TAU = 0.5

F32 = jnp.float32
ANY = pl.BlockSpec(memory_space=pl.ANY)
VM = pl.BlockSpec(memory_space=pltpu.VMEM)
SM = pl.BlockSpec(memory_space=pltpu.SMEM)


def call(kernel, args, outs, name, aliases=None, sems=0, flops=1 << 20, scratch=()):
    specs = {"vmem": VM, "hbm": ANY, "smem": SM}
    spaces = {"vmem": pltpu.VMEM, "hbm": pltpu.HBM}
    operands = [
        pltpu.with_memory_space_constraint(a, spaces[k]) if k in spaces else a for k, a in args
    ]
    shapes = [
        pltpu.VMEM(s, t) if k == "vmem" else jax.ShapeDtypeStruct(s, t) for k, s, t in outs
    ]
    return pl.pallas_call(
        kernel,
        out_shape=shapes,
        in_specs=[specs[k] for k, _ in args],
        out_specs=[specs[k] for k, _, _ in outs],
        input_output_aliases=aliases or {},
        scratch_shapes=list(scratch) + [pltpu.SemaphoreType.DMA((sems,))],
        cost_estimate=pl.CostEstimate(
            flops=flops, bytes_accessed=4 << 20, transcendentals=0
        ),
        compiler_params=pltpu.CompilerParams(vmem_limit_bytes=8 << 20),
        name=name,
    )(*operands)


def copies_of(pairs, sems, first=0):
    return [
        pltpu.make_async_copy(s, d, sems.at[first + i]) for i, (s, d) in enumerate(pairs)
    ]


def start_all(copies):
    for copy in copies:
        copy.start()


def wait_all(copies):
    for copy in copies:
        copy.wait()


def sweep(low, high, tiles, cell, limit=UNROLL):
    rows = high - low
    group = max(g for g in range(1, rows + 1) if rows % g == 0 and g * len(tiles) <= limit)

    def some(i, carry):
        for k in range(group):
            for y in tiles:
                cell(low + i * group + k, y)
        return carry

    if group == rows:
        some(0, 0)
    else:
        lax.fori_loop(0, rows // group, some, 0)


def odd_brick():
    return lax.axis_index("brick") % 2


def pack_kernel(vel, press, level, x_in, x_out, y_lo, y_hi, V, L, R, sems):
    size_x, size_y = level.shape[:2]
    odd = odd_brick()
    inner = pl.ds(RIM, size_x)

    def part(first, count):
        rows, place = pl.ds(first, count), pl.ds(LEFT + first, count)
        return [
            (level.at[:, rows], L.at[inner, place]),
            (vel.at[:, :, rows], V.at[:, inner, place]),
            (press.at[:, rows], R.at[inner, place]),
        ]

    strips = part(0, 8) + part(size_y - 8, 8)
    rest = []
    for out, high in ((x_in, 1 - odd), (x_out, odd)):
        def rows(n):
            return pl.ds(high * (size_x - n), n)

        rest.append((level.at[rows(RIM)], out.at[pl.ds(0, RIM)]))
        for i in range(3):
            rest.append((vel.at[i, rows(DEEP)], out.at[pl.ds(RIM + i * DEEP, DEEP)]))
        rest.append((press.at[rows(1)], out.at[pl.ds(RIM + 3 * DEEP, 1)]))
    rest += part(8, size_y - 16)[:2]
    strips = copies_of(strips, sems)
    rest = copies_of(rest, sems, len(strips))
    start_all(strips + rest)

    def gather(out, high, x, y):
        row = (x - RIM) * SLABS

        def take(ref, n, place, *lead):
            start = LEFT + (size_y - n if high else 0)
            out[pl.ds(row + place, n), :] = ref[(*lead, x, pl.ds(start, n), slice(None))]

        take(L, RIM, 0)
        for i in range(3):
            take(V, DEEP, RIM + i * DEEP, i)
        take(R, 1, RIM + 3 * DEEP)

    for high, out in enumerate((y_lo, y_hi)):
        wait_all(strips[3 * high : 3 * high + 3])
        sweep(RIM, RIM + size_x, [0], functools.partial(gather, out, high), 16)
    wait_all(rest)


def relay_kernel(after, q_lo, q_hi, z_in, z_out, sems):
    rows = q_lo.shape[0]
    odd = odd_brick()
    pairs = []
    for out, high in ((z_in, 1 - odd), (z_out, odd)):
        start = pl.multiple_of(high * (rows - CORNER), 8)
        for side, q in enumerate((q_lo, q_hi)):
            pairs.append((q.at[pl.ds(start, CORNER)], out.at[side]))
    copies = copies_of(pairs, sems)
    start_all(copies)
    wait_all(copies)


def turn(value):
    return pltpu.roll(value, 1, 1), pltpu.roll(value, value.shape[1] - 1, 1)


def tile(ref, x, y, *lead):
    return ref[(*lead, x, pl.ds(y, 8), slice(None))]


def predict(V, R, K, VS, x, y):
    kinds = tile(K, x - RIM, y - LEFT)
    rm, rp = turn(tile(R, x, y))
    grads = (
        tile(R, x + 1, y) - tile(R, x - 1, y),
        tile(R, x, y + 1) - tile(R, x, y - 1),
        rp - rm,
    )
    speed = [tile(V, x, y, i) for i in range(3)]
    for i in range(3):
        zm, zp = turn(speed[i])
        plus = (tile(V, x + 1, y, i), tile(V, x, y + 1, i), zp)
        minus = (tile(V, x - 1, y, i), tile(V, x, y - 1, i), zm)
        total = (plus[0] + minus[0]) + (plus[1] + minus[1]) + (plus[2] + minus[2])
        conv = (
            speed[0] * (plus[0] - minus[0])
            + speed[1] * (plus[1] - minus[1])
            + speed[2] * (plus[2] - minus[2])
        )
        pred = (1.0 - 6.0 * DT * VISC) * speed[i] + (
            DT * VISC * total - 0.5 * DT * (conv + grads[i])
        )
        mean = total * (1.0 / 6.0)
        VS[i, x - RIM, pl.ds(y - LEFT, 8), :] = jnp.where(
            kinds == 1, mean, jnp.where(kinds == 2, 0.0, pred)
        )


def advect(L, V, A, S, x, y):
    c = tile(L, x, y)
    zm, zp = turn(c)
    v = [tile(V, x, y, i) for i in range(3)]
    flux = None
    for u, m, p in (
        (v[0], tile(L, x - 1, y), tile(L, x + 1, y)),
        (v[1], tile(L, x, y - 1), tile(L, x, y + 1)),
        (v[2], zm, zp),
    ):
        term = u * jnp.where(u > 0, c - m, p - c)
        flux = term if flux is None else flux + term
    psi = c - DT_SET * flux
    A[x, pl.ds(y, 8), :] = psi
    S[x, pl.ds(y, 8), :] = (TAU * psi) * lax.rsqrt(psi * psi + 1.0)


def evolved(ref, S, x, y):
    c = tile(ref, x, y)
    s = tile(S, x, y)
    zm, zp = turn(c)
    up = s > 0
    g = None
    for m, p in (
        (tile(ref, x - 1, y), tile(ref, x + 1, y)),
        (tile(ref, x, y - 1), tile(ref, x, y + 1)),
        (zm, zp),
    ):
        low = c - jnp.minimum(jnp.minimum(m, p), c)
        high = jnp.maximum(jnp.maximum(m, p), c) - c
        d = jnp.where(up, low, high)
        g = d * d if g is None else g + d * d
    return c - s * (g * lax.rsqrt(g + 1e-30) - 1.0)


def evolve(source, target, S, x, y):
    target[x, pl.ds(y, 8), :] = evolved(source, S, x, y)


def finish(source, S, L, M, F, size_y, x, y):
    new = evolved(source, S, x, y)
    y0 = max(y, LEFT)
    y1 = min(y + 8, LEFT + size_y)
    wide = size_y // BS
    first = (y0 - LEFT) // BS
    last = (y1 - 1 - LEFT) // BS
    mark = M[(x - RIM) // BS * wide + first]
    if first != last:
        edge = LEFT + last * BS - y
        rows = lax.broadcasted_iota(jnp.int32, mark.shape, 0)
        mark = jnp.where(rows < edge, mark, M[(x - RIM) // BS * wide + last])
    value = jnp.where(mark > 0.5, new, tile(L, x, y))
    F[x - RIM, pl.ds(y0 - LEFT, y1 - y0), :] = value[y0 - y : y1 - y]


def inner_kernel(
    V, L, press, overset, count, band_ids, _, R, K, VS, A, S, B, C, F, M, ids, sems
):
    size_x, size_y, size_z = F.shape
    middle = size_y - 16
    named = copies_of([(band_ids, ids)], sems)
    later = copies_of(
        [
            (press.at[:, pl.ds(8, middle)], R.at[pl.ds(RIM, size_x), pl.ds(LEFT + 8, middle)]),
            (overset, K),
        ],
        sems,
        1,
    )
    start_all(named + later)
    core = [LEFT + y for y in range(0, size_y, 8)]
    mid = [LEFT + y for y in range(RIM, size_y - RIM, 8)]
    low, high = RIM, RIM + size_x
    sweep(low + 1, high - 1, core, functools.partial(advect, L, V, A, S))
    sweep(low + 2, high - 2, core, functools.partial(evolve, A, B, S))
    sweep(low + 3, high - 3, core, functools.partial(evolve, B, C, S))

    wait_all(named)
    wide = size_y // BS
    deep = size_z // BS
    lane = lax.broadcasted_iota(jnp.int32, (8, size_z), 1) // BS
    marks = [jnp.zeros((8, size_z), jnp.bool_) for _ in range(size_x // BS * wide)]
    held = count[0, 0]
    for s in range(MAXB):
        block = jnp.where(s < held, ids[0, 0, s], -1)
        marks = [m | (lane == block - k * deep) for k, m in enumerate(marks)]
    for k, m in enumerate(marks):
        M[k] = m.astype(F32)

    sweep(low + 4, high - 4, mid, functools.partial(finish, C, S, L, M, F, size_y))
    wait_all(later)
    sweep(low + 1, high - 1, core[1:-1], functools.partial(predict, V, R, K, VS))


def edge_kernel(
    K, M, x_in, x_out, q_lo, q_hi, *refs
):
    V, L, R, VS, A, S, B, C, F, star, sems = refs[9:]
    size_x, size_y = F.shape[:2]
    body = pl.ds(LEFT, size_y)
    low, high = RIM, RIM + size_x
    odd = odd_brick()
    pairs = []
    for x, upper in ((x_in, 1 - odd), (x_out, odd)):
        place = upper * high + (1 - upper) * (low - RIM)
        pairs.append((x.at[pl.ds(0, RIM)], L.at[pl.ds(place, RIM), body]))
        place = upper * high + (1 - upper) * (low - DEEP)
        for i in range(3):
            pairs.append(
                (x.at[pl.ds(RIM + i * DEEP, DEEP)], V.at[i, pl.ds(place, DEEP), body])
            )
        place = upper * high + (1 - upper) * (low - 1)
        pairs.append((x.at[pl.ds(RIM + 3 * DEEP, 1)], R.at[pl.ds(place, 1), body]))
    copies = copies_of(pairs, sems)
    start_all(copies)

    def spread(x, y):
        for side, q in enumerate((q_lo, q_hi)):
            fill(L, V, x, side, q, (), (x - RIM) * SLABS, size_y)
            place = LEFT + size_y if side else LEFT - 1
            R[x, pl.ds(place, 1), :] = q[pl.ds((x - RIM) * SLABS + RIM + 3 * DEEP, 1), :]

    sweep(low, high, [0], spread, 16)
    wait_all(copies)

    core = [LEFT + y for y in range(0, size_y, 8)]
    mid = [LEFT + y for y in range(RIM, size_y - RIM, 8)]
    outer = [LEFT - RIM, LEFT + size_y - RIM]
    step = functools.partial(predict, V, R, K, VS)
    sweep(low + 1, high - 1, [core[0], core[-1]], step)
    for x in (low, high - 1):
        for y in core:
            step(x, y)
    out = copies_of([(VS.at[i], star.at[i]) for i in range(3)], sems, len(copies))
    start_all(out)

    def ring(depth, cell):
        sweep(low - depth, high + depth, outer, cell)
        sweep(low - depth, low - depth + 4, mid, cell)
        sweep(high + depth - 4, high + depth, mid, cell)

    ring(3, functools.partial(advect, L, V, A, S))
    ring(2, functools.partial(evolve, A, B, S))
    ring(1, functools.partial(evolve, B, C, S))
    ring(0, functools.partial(finish, C, S, L, M, F, size_y))
    wait_all(out)


def fill(L, V, x, side, ref, lead, first, size_y):
    place = LEFT + size_y if side else LEFT - RIM
    L[x, pl.ds(place, RIM), :] = ref[(*lead, pl.ds(first, RIM), slice(None))]
    place = LEFT + size_y if side else LEFT - DEEP
    for i in range(3):
        V[i, x, pl.ds(place, DEEP), :] = ref[
            (*lead, pl.ds(first + RIM + i * DEEP, DEEP), slice(None))
        ]


def corner_kernel(M, z_in, z_out, *refs):
    V, L, A, S, B, C, F, new, sems = refs[7:]
    size_x, size_y = F.shape[:2]
    low, high = RIM, RIM + size_x
    early = copies_of(
        [(F.at[pl.ds(3, size_x - 6)], new.at[pl.ds(3, size_x - 6)])], sems
    )
    start_all(early)
    skipped = CORNER - DEEP * SLABS
    odd = odd_brick()
    for z, upper in ((z_in, 1 - odd), (z_out, odd)):
        place = upper * high + (1 - upper) * (low - DEEP)
        first = (1 - upper) * skipped
        for k in range(DEEP):
            for side in range(2):
                fill(L, V, place + k, side, z, (side,), first + k * SLABS, size_y)

    outer = [LEFT - RIM, LEFT + size_y - RIM]

    def ends(depth, cell):
        rows = 4 if depth else 3
        for k in range(rows):
            for x in (low - depth + k, high + depth - 1 - k):
                for y in outer:
                    cell(x, y)

    ends(3, functools.partial(advect, L, V, A, S))
    ends(2, functools.partial(evolve, A, B, S))
    ends(1, functools.partial(evolve, B, C, S))
    ends(0, functools.partial(finish, C, S, L, M, F, size_y))
    late = copies_of(
        [(F.at[pl.ds(x, 3)], new.at[pl.ds(x, 3)]) for x in (0, size_x - 3)], sems, 1
    )
    start_all(late)
    wait_all(early + late)


def moved(array, axis, step):
    peers = lax.axis_size(axis)
    return lax.ppermute(array, axis, [(i, (i + step) % peers) for i in range(peers)])


def swapped(array, axis, shift):
    peers = lax.axis_size(axis)
    pairs = [(i, (((i + shift) ^ 1) - shift) % peers) for i in range(peers)]
    return lax.ppermute(array, axis, pairs)


def shards(velocity, pressure, level_set, overset, band_count, band_ids):
    size_x, size_y, size_z = level_set.shape
    plain = level_set.shape
    padded = (size_x + 2 * RIM, LEFT + size_y + 8, size_z)
    x_face = (SLABS, size_y, size_z)
    y_face = (size_x * SLABS, size_z)
    marks = (size_x // BS * (size_y // BS), 8, size_z)

    x_in, x_out, y_low, y_high, V, L, R = call(
        pack_kernel,
        [("hbm", velocity), ("hbm", pressure), ("hbm", level_set)],
        [("vmem", x_face, F32)] * 2
        + [("vmem", y_face, F32)] * 2
        + [("vmem", (3,) + padded, F32), ("vmem", padded, F32), ("vmem", padded, F32)],
        "pack",
        sems=24,
    )
    q_lo = moved(y_high, "col", 1)
    q_hi = moved(y_low, "col", -1)
    x_in = swapped(x_in, "brick", 0)
    x_out = swapped(x_out, "brick", 1)
    R, K, VS, A, S, B, C, F, M = call(
        inner_kernel,
        [("vmem", V), ("vmem", L), ("hbm", pressure), ("hbm", overset)]
        + [("smem", band_count), ("hbm", band_ids), ("vmem", R)],
        [("vmem", padded, F32), ("vmem", plain, jnp.int32), ("vmem", (3,) + plain, F32)]
        + [("vmem", padded, F32)] * 4
        + [("vmem", plain, F32), ("vmem", marks, F32)],
        "inner",
        aliases={6: 0},
        scratch=[pltpu.SMEM(band_ids.shape, jnp.int32)],
        sems=3,
        flops=60 << 20,
    )
    z_in, z_out = call(
        relay_kernel,
        [("vmem", M), ("vmem", q_lo), ("vmem", q_hi)],
        [("vmem", (2, CORNER, size_z), F32)] * 2,
        "relay",
        sems=4,
    )
    z_in = swapped(z_in, "brick", 0)
    z_out = swapped(z_out, "brick", 1)
    state = [V, L, R, VS, A, S, B, C, F]
    held = [("vmem", K), ("vmem", M)] + [("vmem", a) for a in (x_in, x_out, q_lo, q_hi)]
    *state, velocity_star = call(
        edge_kernel,
        held + [("vmem", a) for a in state],
        [("vmem", a.shape, F32) for a in state] + [("hbm", velocity.shape, F32)],
        "edge",
        aliases={len(held) + i: i for i in range(len(state))},
        sems=13,
        flops=60 << 20,
    )
    V, L, R, VS, A, S, B, C, F = state
    state = [V, L, A, S, B, C, F]
    held = [("vmem", M), ("vmem", z_in), ("vmem", z_out)]
    *state, level_set_new = call(
        corner_kernel,
        held + [("vmem", a) for a in state],
        [("vmem", a.shape, F32) for a in state] + [("hbm", plain, F32)],
        "corner",
        aliases={len(held) + i: i for i in range(len(state))},
        sems=3,
    )
    return (velocity_star, level_set_new)


def solution(mesh):
    return jax.shard_map(
        shards,
        mesh=mesh,
        in_specs=(
            P(None, "brick", "col", None),
            P("brick", "col", None),
            P("brick", "col", None),
            P("brick", "col", None),
            P("brick", "col"),
            P("brick", "col", None),
        ),
        out_specs=(P(None, "brick", "col", None), P("brick", "col", None)),
        check_vma=False,
    )
```

```python
import functools

import jax
import jax.numpy as jnp
from jax import lax
from jax.experimental import pallas as pl
from jax.experimental.pallas import tpu as pltpu
from jax.sharding import PartitionSpec as P

BS = 16
REINIT = 3
MAXB = 16
RIM = 4
DEEP = 3
SLABS = RIM + 3 * DEEP + 1
CORNER = 32
LEFT = 8
UNROLL = 80

DT = 0.1
VISC = 0.5
DT_SET = 0.2
TAU = 0.5

F32 = jnp.float32
ANY = pl.BlockSpec(memory_space=pl.ANY)
VM = pl.BlockSpec(memory_space=pltpu.VMEM)
SM = pl.BlockSpec(memory_space=pltpu.SMEM)


def call(kernel, args, outs, name, aliases=None, sems=0, flops=1 << 20, scratch=()):
    specs = {"vmem": VM, "hbm": ANY, "smem": SM}
    spaces = {"vmem": pltpu.VMEM, "hbm": pltpu.HBM}
    operands = [
        pltpu.with_memory_space_constraint(a, spaces[k]) if k in spaces else a for k, a in args
    ]
    shapes = [
        pltpu.VMEM(s, t) if k == "vmem" else jax.ShapeDtypeStruct(s, t) for k, s, t in outs
    ]
    return pl.pallas_call(
        kernel,
        out_shape=shapes,
        in_specs=[specs[k] for k, _ in args],
        out_specs=[specs[k] for k, _, _ in outs],
        input_output_aliases=aliases or {},
        scratch_shapes=list(scratch) + [pltpu.SemaphoreType.DMA((sems,))],
        cost_estimate=pl.CostEstimate(
            flops=flops, bytes_accessed=4 << 20, transcendentals=0
        ),
        compiler_params=pltpu.CompilerParams(vmem_limit_bytes=8 << 20),
        name=name,
    )(*operands)


def copies_of(pairs, sems, first=0):
    return [
        pltpu.make_async_copy(s, d, sems.at[first + i]) for i, (s, d) in enumerate(pairs)
    ]


def start_all(copies):
    for copy in copies:
        copy.start()


def wait_all(copies):
    for copy in copies:
        copy.wait()


def sweep(low, high, tiles, cell, limit=UNROLL):
    rows = high - low
    group = max(g for g in range(1, rows + 1) if rows % g == 0 and g * len(tiles) <= limit)

    def some(i, carry):
        for k in range(group):
            for y in tiles:
                cell(low + i * group + k, y)
        return carry

    if group == rows:
        some(0, 0)
    else:
        lax.fori_loop(0, rows // group, some, 0)


def odd_brick():
    return lax.axis_index("brick") % 2


def pack_kernel(vel, press, level, x_in, x_out, y_lo, y_hi, V, L, R, sems):
    size_x, size_y = level.shape[:2]
    odd = odd_brick()
    inner = pl.ds(RIM, size_x)

    def part(first, count):
        rows, place = pl.ds(first, count), pl.ds(LEFT + first, count)
        return [
            (level.at[:, rows], L.at[inner, place]),
            (vel.at[:, :, rows], V.at[:, inner, place]),
            (press.at[:, rows], R.at[inner, place]),
        ]

    strips = part(0, 8) + part(size_y - 8, 8)
    rest = []
    for out, high in ((x_in, 1 - odd), (x_out, odd)):
        def rows(n):
            return pl.ds(high * (size_x - n), n)

        rest.append((level.at[rows(RIM)], out.at[pl.ds(0, RIM)]))
        for i in range(3):
            rest.append((vel.at[i, rows(DEEP)], out.at[pl.ds(RIM + i * DEEP, DEEP)]))
        rest.append((press.at[rows(1)], out.at[pl.ds(RIM + 3 * DEEP, 1)]))
    rest += part(8, size_y - 16)[:2]
    strips = copies_of(strips, sems)
    rest = copies_of(rest, sems, len(strips))
    start_all(strips + rest)

    def put(out, row, ref, x, y, n, *lead):
        out[pl.ds(row, n), :] = ref[(*lead, x, pl.ds(LEFT + y, n), slice(None))]

    def gather(out, high, x, y):
        row = 8 * (x - RIM + 1)
        near = size_y - 1 if high else 0
        put(out, row, L, x, size_y - 2 if high else 0, 2)
        first = size_y - 7 if high else -1
        psi = advected(L, V, x, LEFT + first)
        place = (size_y - 3 if high else 1) - first
        out[pl.ds(row + 2, 2), :] = psi[place : place + 2]
        for i in range(3):
            put(out, row + 4 + i, V, x, near, 1, i)
        put(out, row + 7, R, x, near, 1)

    for high, out in enumerate((y_lo, y_hi)):
        wait_all(strips[3 * high : 3 * high + 3])
        sweep(RIM, RIM + size_x, [0], functools.partial(gather, out, high), 16)
        for x, near, more in (
            (RIM, RIM + 1, 0),
            (RIM + size_x - 1, RIM + size_x - 2, 8 * (size_x + 1)),
        ):
            put(out, 8 * (x - RIM + 1) + 2, L, x, size_y - 4 if high else 2, 2)
            put(out, more, L, near, size_y - 3 if high else 2, 1)
            for i in range(3):
                put(out, more + 1 + 2 * i, V, x, size_y - 3 if high else 1, 2, i)
    wait_all(rest)


def fill(L, V, x, side, ref, lead, row, size_y):
    place = LEFT + size_y if side else LEFT - 2
    L[x, pl.ds(place, 2), :] = ref[(*lead, pl.ds(row, 2), slice(None))]
    place = LEFT + size_y if side else LEFT - 1
    for i in range(3):
        V[i, x, pl.ds(place, 1), :] = ref[(*lead, pl.ds(row + 4 + i, 1), slice(None))]


def fill_raw(L, V, x, side, ref, lead, row, more, size_y):
    place = LEFT + size_y + 2 if side else LEFT - 4
    L[x, pl.ds(place, 2), :] = ref[(*lead, pl.ds(row + 2, 2), slice(None))]
    place = LEFT + size_y + 1 if side else LEFT - 3
    for i in range(3):
        V[i, x, pl.ds(place, 2), :] = ref[(*lead, pl.ds(more + 1 + 2 * i, 2), slice(None))]


def relay_kernel(after, q_lo, q_hi, z_in, z_out, sems):
    rows = q_lo.shape[0]
    odd = odd_brick()
    pairs = []
    for out, high in ((z_in, 1 - odd), (z_out, odd)):
        start = pl.multiple_of(high * (rows - CORNER), 8)
        for side, q in enumerate((q_lo, q_hi)):
            pairs.append((q.at[pl.ds(start, CORNER)], out.at[side]))
    copies = copies_of(pairs, sems)
    start_all(copies)
    wait_all(copies)


def turn(value):
    return pltpu.roll(value, 1, 1), pltpu.roll(value, value.shape[1] - 1, 1)


def tile(ref, x, y, *lead):
    return ref[(*lead, x, pl.ds(y, 8), slice(None))]


def predict(V, R, K, VS, x, y):
    kinds = tile(K, x - RIM, y - LEFT)
    rm, rp = turn(tile(R, x, y))
    grads = (
        tile(R, x + 1, y) - tile(R, x - 1, y),
        tile(R, x, y + 1) - tile(R, x, y - 1),
        rp - rm,
    )
    speed = [tile(V, x, y, i) for i in range(3)]
    for i in range(3):
        zm, zp = turn(speed[i])
        plus = (tile(V, x + 1, y, i), tile(V, x, y + 1, i), zp)
        minus = (tile(V, x - 1, y, i), tile(V, x, y - 1, i), zm)
        total = (plus[0] + minus[0]) + (plus[1] + minus[1]) + (plus[2] + minus[2])
        conv = (
            speed[0] * (plus[0] - minus[0])
            + speed[1] * (plus[1] - minus[1])
            + speed[2] * (plus[2] - minus[2])
        )
        pred = (1.0 - 6.0 * DT * VISC) * speed[i] + (
            DT * VISC * total - 0.5 * DT * (conv + grads[i])
        )
        mean = total * (1.0 / 6.0)
        VS[i, x - RIM, pl.ds(y - LEFT, 8), :] = jnp.where(
            kinds == 1, mean, jnp.where(kinds == 2, 0.0, pred)
        )


def advected(L, V, x, y):
    c = tile(L, x, y)
    zm, zp = turn(c)
    v = [tile(V, x, y, i) for i in range(3)]
    flux = None
    for u, m, p in (
        (v[0], tile(L, x - 1, y), tile(L, x + 1, y)),
        (v[1], tile(L, x, y - 1), tile(L, x, y + 1)),
        (v[2], zm, zp),
    ):
        term = u * jnp.where(u > 0, c - m, p - c)
        flux = term if flux is None else flux + term
    return c - DT_SET * flux


def scaled_sign(psi):
    return (TAU * psi) * lax.rsqrt(psi * psi + 1.0)


def advect(L, V, A, S, x, y):
    psi = advected(L, V, x, y)
    A[x, pl.ds(y, 8), :] = psi
    S[x, pl.ds(y, 8), :] = scaled_sign(psi)


def evolved(ref, S, x, y):
    c = tile(ref, x, y)
    s = tile(S, x, y)
    zm, zp = turn(c)
    up = s > 0
    g = None
    for m, p in (
        (tile(ref, x - 1, y), tile(ref, x + 1, y)),
        (tile(ref, x, y - 1), tile(ref, x, y + 1)),
        (zm, zp),
    ):
        low = c - jnp.minimum(jnp.minimum(m, p), c)
        high = jnp.maximum(jnp.maximum(m, p), c) - c
        d = jnp.where(up, low, high)
        g = d * d if g is None else g + d * d
    return c - s * (g * lax.rsqrt(g + 1e-30) - 1.0)


def evolve(source, target, S, x, y):
    target[x, pl.ds(y, 8), :] = evolved(source, S, x, y)


def finish(source, S, L, M, F, size_y, x, y):
    new = evolved(source, S, x, y)
    y0 = max(y, LEFT)
    y1 = min(y + 8, LEFT + size_y)
    wide = size_y // BS
    first = (y0 - LEFT) // BS
    last = (y1 - 1 - LEFT) // BS
    mark = M[(x - RIM) // BS * wide + first]
    if first != last:
        edge = LEFT + last * BS - y
        rows = lax.broadcasted_iota(jnp.int32, mark.shape, 0)
        mark = jnp.where(rows < edge, mark, M[(x - RIM) // BS * wide + last])
    value = jnp.where(mark > 0.5, new, tile(L, x, y))
    F[x - RIM, pl.ds(y0 - LEFT, y1 - y0), :] = value[y0 - y : y1 - y]


def inner_kernel(
    V, L, press, overset, count, band_ids, _, R, K, VS, A, S, B, C, F, M, ids, sems
):
    size_x, size_y, size_z = F.shape
    middle = size_y - 16
    named = copies_of([(band_ids, ids)], sems)
    later = copies_of(
        [
            (press.at[:, pl.ds(8, middle)], R.at[pl.ds(RIM, size_x), pl.ds(LEFT + 8, middle)]),
            (overset, K),
        ],
        sems,
        1,
    )
    start_all(named + later)
    core = [LEFT + y for y in range(0, size_y, 8)]
    mid = [LEFT + y for y in range(RIM, size_y - RIM, 8)]
    low, high = RIM, RIM + size_x
    sweep(low + 1, high - 1, core, functools.partial(advect, L, V, A, S))
    sweep(low + 2, high - 2, core, functools.partial(evolve, A, B, S))
    sweep(low + 3, high - 3, core, functools.partial(evolve, B, C, S))

    wait_all(named)
    wide = size_y // BS
    deep = size_z // BS
    lane = lax.broadcasted_iota(jnp.int32, (8, size_z), 1) // BS
    marks = [jnp.zeros((8, size_z), jnp.bool_) for _ in range(size_x // BS * wide)]
    held = count[0, 0]
    for s in range(MAXB):
        block = jnp.where(s < held, ids[0, 0, s], -1)
        marks = [m | (lane == block - k * deep) for k, m in enumerate(marks)]
    for k, m in enumerate(marks):
        M[k] = m.astype(F32)

    sweep(low + 4, high - 4, mid, functools.partial(finish, C, S, L, M, F, size_y))
    wait_all(later)
    sweep(low + 1, high - 1, core[1:-1], functools.partial(predict, V, R, K, VS))


def edge_kernel(
    K, M, x_in, x_out, q_lo, q_hi, *refs
):
    V, L, R, VS, A, S, B, C, F, star, sems = refs[9:]
    size_x, size_y = F.shape[:2]
    body = pl.ds(LEFT, size_y)
    low, high = RIM, RIM + size_x
    odd = odd_brick()
    pairs = []
    for x, upper in ((x_in, 1 - odd), (x_out, odd)):
        place = upper * high + (1 - upper) * (low - RIM)
        pairs.append((x.at[pl.ds(0, RIM)], L.at[pl.ds(place, RIM), body]))
        place = upper * high + (1 - upper) * (low - DEEP)
        for i in range(3):
            pairs.append(
                (x.at[pl.ds(RIM + i * DEEP, DEEP)], V.at[i, pl.ds(place, DEEP), body])
            )
        place = upper * high + (1 - upper) * (low - 1)
        pairs.append((x.at[pl.ds(RIM + 3 * DEEP, 1)], R.at[pl.ds(place, 1), body]))
    copies = copies_of(pairs, sems)
    start_all(copies)

    def spread(x, y):
        row = 8 * (x - RIM + 1)
        for side, q in enumerate((q_lo, q_hi)):
            fill(L, V, x, side, q, (), row, size_y)
            place = LEFT + size_y if side else LEFT - 1
            R[x, pl.ds(place, 1), :] = q[pl.ds(row + 7, 1), :]

    sweep(low, high, [0], spread, 16)
    for side, q in enumerate((q_lo, q_hi)):
        place = LEFT + size_y + 2 if side else LEFT - 3
        for x, near, more in ((low, low + 1, 0), (high - 1, high - 2, 8 * (size_x + 1))):
            fill_raw(L, V, x, side, q, (), 8 * (x - RIM + 1), more, size_y)
            L[near, pl.ds(place, 1), :] = q[pl.ds(more, 1), :]
    wait_all(copies)

    core = [LEFT + y for y in range(0, size_y, 8)]
    mid = [LEFT + y for y in range(RIM, size_y - RIM, 8)]
    outer = [LEFT - RIM, LEFT + size_y - RIM]
    step = functools.partial(predict, V, R, K, VS)
    sweep(low + 1, high - 1, [core[0], core[-1]], step)
    for x in (low, high - 1):
        for y in core:
            step(x, y)
    out = copies_of([(VS.at[i], star.at[i]) for i in range(3)], sems, len(copies))
    start_all(out)

    def ring(depth, cell):
        sweep(low - depth, high + depth, outer, cell)
        sweep(low - depth, low - depth + 4, mid, cell)
        sweep(high + depth - 4, high + depth, mid, cell)

    ring(3, functools.partial(advect, L, V, A, S))

    def take(x, y):
        for side, q in enumerate((q_lo, q_hi)):
            psi = q[pl.ds(8 * (x - RIM + 1) + 2, 2), :]
            place = pl.ds(LEFT + size_y + 1 if side else LEFT - 3, 2)
            A[x, place, :] = psi
            S[x, place, :] = scaled_sign(psi)

    sweep(low + 1, high - 1, [0], take, 16)
    ring(2, functools.partial(evolve, A, B, S))
    ring(1, functools.partial(evolve, B, C, S))
    ring(0, functools.partial(finish, C, S, L, M, F, size_y))
    wait_all(out)


def corner_kernel(M, z_in, z_out, *refs):
    V, L, A, S, B, C, F, new, sems = refs[7:]
    size_x, size_y = F.shape[:2]
    low, high = RIM, RIM + size_x
    early = copies_of(
        [(F.at[pl.ds(3, size_x - 6)], new.at[pl.ds(3, size_x - 6)])], sems
    )
    start_all(early)
    odd = odd_brick()
    for z, upper in ((z_in, 1 - odd), (z_out, odd)):
        place = upper * high + (1 - upper) * (low - DEEP)
        edge = upper * high + (1 - upper) * (low - 1)
        first = upper * 8
        for side in range(2):
            for k in range(DEEP):
                fill(L, V, place + k, side, z, (side,), first + k * 8, size_y)
            fill_raw(
                L, V, edge, side, z, (side,), 16 - upper * 8, 24 - upper * 24, size_y
            )

    outer = [LEFT - RIM, LEFT + size_y - RIM]

    def ends(depth, cell):
        rows = 4 if depth else 3
        for k in range(rows):
            for x in (low - depth + k, high + depth - 1 - k):
                for y in outer:
                    cell(x, y)

    ends(3, functools.partial(advect, L, V, A, S))
    ends(2, functools.partial(evolve, A, B, S))
    ends(1, functools.partial(evolve, B, C, S))
    ends(0, functools.partial(finish, C, S, L, M, F, size_y))
    late = copies_of(
        [(F.at[pl.ds(x, 3)], new.at[pl.ds(x, 3)]) for x in (0, size_x - 3)], sems, 1
    )
    start_all(late)
    wait_all(early + late)


def moved(array, axis, step):
    peers = lax.axis_size(axis)
    return lax.ppermute(array, axis, [(i, (i + step) % peers) for i in range(peers)])


def swapped(array, axis, shift):
    peers = lax.axis_size(axis)
    pairs = [(i, (((i + shift) ^ 1) - shift) % peers) for i in range(peers)]
    return lax.ppermute(array, axis, pairs)


def shards(velocity, pressure, level_set, overset, band_count, band_ids):
    size_x, size_y, size_z = level_set.shape
    plain = level_set.shape
    padded = (size_x + 2 * RIM, LEFT + size_y + 8, size_z)
    x_face = (SLABS, size_y, size_z)
    y_face = ((size_x + 2) * 8, size_z)
    marks = (size_x // BS * (size_y // BS), 8, size_z)

    x_in, x_out, y_low, y_high, V, L, R = call(
        pack_kernel,
        [("hbm", velocity), ("hbm", pressure), ("hbm", level_set)],
        [("vmem", x_face, F32)] * 2
        + [("vmem", y_face, F32)] * 2
        + [("vmem", (3,) + padded, F32), ("vmem", padded, F32), ("vmem", padded, F32)],
        "pack",
        sems=24,
    )
    q_lo = moved(y_high, "col", 1)
    q_hi = moved(y_low, "col", -1)
    x_in = swapped(x_in, "brick", 0)
    x_out = swapped(x_out, "brick", 1)
    R, K, VS, A, S, B, C, F, M = call(
        inner_kernel,
        [("vmem", V), ("vmem", L), ("hbm", pressure), ("hbm", overset)]
        + [("smem", band_count), ("hbm", band_ids), ("vmem", R)],
        [("vmem", padded, F32), ("vmem", plain, jnp.int32), ("vmem", (3,) + plain, F32)]
        + [("vmem", padded, F32)] * 4
        + [("vmem", plain, F32), ("vmem", marks, F32)],
        "inner",
        aliases={6: 0},
        scratch=[pltpu.SMEM(band_ids.shape, jnp.int32)],
        sems=3,
        flops=60 << 20,
    )
    z_in, z_out = call(
        relay_kernel,
        [("vmem", M), ("vmem", q_lo), ("vmem", q_hi)],
        [("vmem", (2, CORNER, size_z), F32)] * 2,
        "relay",
        sems=4,
    )
    z_in = swapped(z_in, "brick", 0)
    z_out = swapped(z_out, "brick", 1)
    state = [V, L, R, VS, A, S, B, C, F]
    held = [("vmem", K), ("vmem", M)] + [("vmem", a) for a in (x_in, x_out, q_lo, q_hi)]
    *state, velocity_star = call(
        edge_kernel,
        held + [("vmem", a) for a in state],
        [("vmem", a.shape, F32) for a in state] + [("hbm", velocity.shape, F32)],
        "edge",
        aliases={len(held) + i: i for i in range(len(state))},
        sems=13,
        flops=60 << 20,
    )
    V, L, R, VS, A, S, B, C, F = state
    state = [V, L, A, S, B, C, F]
    held = [("vmem", M), ("vmem", z_in), ("vmem", z_out)]
    *state, level_set_new = call(
        corner_kernel,
        held + [("vmem", a) for a in state],
        [("vmem", a.shape, F32) for a in state] + [("hbm", plain, F32)],
        "corner",
        aliases={len(held) + i: i for i in range(len(state))},
        sems=3,
    )
    return (velocity_star, level_set_new)


def solution(mesh):
    return jax.shard_map(
        shards,
        mesh=mesh,
        in_specs=(
            P(None, "brick", "col", None),
            P("brick", "col", None),
            P("brick", "col", None),
            P("brick", "col", None),
            P("brick", "col"),
            P("brick", "col", None),
        ),
        out_specs=(P(None, "brick", "col", None), P("brick", "col", None)),
        check_vma=False,
    )
```

```python
import functools

import jax
import jax.numpy as jnp
from jax import lax
from jax.experimental import pallas as pl
from jax.experimental.pallas import tpu as pltpu
from jax.sharding import PartitionSpec as P

BS = 16
REINIT = 3
MAXB = 16
RIM = 4
DEEP = 3
SLABS = RIM + 3 * DEEP + 1
CORNER = 32
LEFT = 8
UNROLL = 80

DT = 0.1
VISC = 0.5
DT_SET = 0.2
TAU = 0.5

F32 = jnp.float32
ANY = pl.BlockSpec(memory_space=pl.ANY)
VM = pl.BlockSpec(memory_space=pltpu.VMEM)
SM = pl.BlockSpec(memory_space=pltpu.SMEM)


def call(kernel, args, outs, name, aliases=None, sems=0, flops=1 << 20, scratch=()):
    specs = {"vmem": VM, "hbm": ANY, "smem": SM}
    spaces = {"vmem": pltpu.VMEM, "hbm": pltpu.HBM}
    operands = [
        pltpu.with_memory_space_constraint(a, spaces[k]) if k in spaces else a for k, a in args
    ]
    shapes = [
        pltpu.VMEM(s, t) if k == "vmem" else jax.ShapeDtypeStruct(s, t) for k, s, t in outs
    ]
    return pl.pallas_call(
        kernel,
        out_shape=shapes,
        in_specs=[specs[k] for k, _ in args],
        out_specs=[specs[k] for k, _, _ in outs],
        input_output_aliases=aliases or {},
        scratch_shapes=list(scratch) + [pltpu.SemaphoreType.DMA((sems,))],
        cost_estimate=pl.CostEstimate(
            flops=flops, bytes_accessed=4 << 20, transcendentals=0
        ),
        compiler_params=pltpu.CompilerParams(vmem_limit_bytes=8 << 20),
        name=name,
    )(*operands)


def copies_of(pairs, sems, first=0):
    return [
        pltpu.make_async_copy(s, d, sems.at[first + i]) for i, (s, d) in enumerate(pairs)
    ]


def start_all(copies):
    for copy in copies:
        copy.start()


def wait_all(copies):
    for copy in copies:
        copy.wait()


def sweep(low, high, tiles, cell, limit=UNROLL):
    rows = high - low
    group = max(g for g in range(1, rows + 1) if rows % g == 0 and g * len(tiles) <= limit)

    def some(i, carry):
        for k in range(group):
            for y in tiles:
                cell(low + i * group + k, y)
        return carry

    if group == rows:
        some(0, 0)
    else:
        lax.fori_loop(0, rows // group, some, 0)


def odd_brick():
    return lax.axis_index("brick") % 2


def pack_kernel(vel, press, level, y_lo, y_hi, V, L, R, sems):
    size_x, size_y = level.shape[:2]
    inner = pl.ds(RIM, size_x)

    def part(first, count):
        rows, place = pl.ds(first, count), pl.ds(LEFT + first, count)
        return [
            (level.at[:, rows], L.at[inner, place]),
            (vel.at[:, :, rows], V.at[:, inner, place]),
            (press.at[:, rows], R.at[inner, place]),
        ]

    strips = part(0, 8) + part(size_y - 8, 8)
    rest = part(8, size_y - 16)[:2]
    strips = copies_of(strips, sems)
    rest = copies_of(rest, sems, len(strips))
    start_all(strips + rest)

    def put(out, row, ref, x, y, n, *lead):
        out[pl.ds(row, n), :] = ref[(*lead, x, pl.ds(LEFT + y, n), slice(None))]

    def gather(out, high, x, y):
        row = 8 * (x - RIM + 1)
        near = size_y - 1 if high else 0
        put(out, row, L, x, size_y - 2 if high else 0, 2)
        first = size_y - 7 if high else -1
        psi = advected(L, V, x, LEFT + first)
        place = (size_y - 3 if high else 1) - first
        out[pl.ds(row + 2, 2), :] = psi[place : place + 2]
        for i in range(3):
            put(out, row + 4 + i, V, x, near, 1, i)
        put(out, row + 7, R, x, near, 1)

    for high, out in enumerate((y_lo, y_hi)):
        wait_all(strips[3 * high : 3 * high + 3])
        sweep(RIM, RIM + size_x, [0], functools.partial(gather, out, high), 16)
        for x, near, more in (
            (RIM, RIM + 1, 0),
            (RIM + size_x - 1, RIM + size_x - 2, 8 * (size_x + 1)),
        ):
            put(out, 8 * (x - RIM + 1) + 2, L, x, size_y - 4 if high else 2, 2)
            put(out, more, L, near, size_y - 3 if high else 2, 1)
            for i in range(3):
                put(out, more + 1 + 2 * i, V, x, size_y - 3 if high else 1, 2, i)
    wait_all(rest)


def fill(L, V, x, side, ref, lead, row, size_y):
    place = LEFT + size_y if side else LEFT - 2
    L[x, pl.ds(place, 2), :] = ref[(*lead, pl.ds(row, 2), slice(None))]
    place = LEFT + size_y if side else LEFT - 1
    for i in range(3):
        V[i, x, pl.ds(place, 1), :] = ref[(*lead, pl.ds(row + 4 + i, 1), slice(None))]


def fill_raw(L, V, x, side, ref, lead, row, more, size_y):
    place = LEFT + size_y + 2 if side else LEFT - 4
    L[x, pl.ds(place, 2), :] = ref[(*lead, pl.ds(row + 2, 2), slice(None))]
    place = LEFT + size_y + 1 if side else LEFT - 3
    for i in range(3):
        V[i, x, pl.ds(place, 2), :] = ref[(*lead, pl.ds(more + 1 + 2 * i, 2), slice(None))]


def relay_kernel(V, L, R, after, q_lo, q_hi, x_in, x_out, sems):
    rows = q_lo.shape[0]
    size_y = x_in.shape[1]
    size_x = L.shape[0] - 2 * RIM
    body = pl.ds(LEFT, size_y)
    odd = odd_brick()
    pairs = []
    for out, high in ((x_in, 1 - odd), (x_out, odd)):
        def edge(n):
            return pl.ds(RIM + high * (size_x - n), n)

        pairs.append((L.at[edge(RIM), body], out.at[pl.ds(0, RIM)]))
        for i in range(3):
            pairs.append((V.at[i, edge(DEEP), body], out.at[pl.ds(RIM + i * DEEP, DEEP)]))
        pairs.append((R.at[edge(1), body], out.at[pl.ds(SLABS - 1, 1)]))
        start = pl.multiple_of(high * (rows - CORNER), 8)
        for side, q in enumerate((q_lo, q_hi)):
            pairs.append(
                (q.at[pl.ds(start, CORNER)], out.at[SLABS + side, pl.ds(0, CORNER)])
            )
    copies = copies_of(pairs, sems)
    start_all(copies)
    wait_all(copies)


def turn(value):
    return pltpu.roll(value, 1, 1), pltpu.roll(value, value.shape[1] - 1, 1)


def tile(ref, x, y, *lead):
    return ref[(*lead, x, pl.ds(y, 8), slice(None))]


def predict(V, R, K, VS, x, y):
    kinds = tile(K, x - RIM, y - LEFT)
    rm, rp = turn(tile(R, x, y))
    grads = (
        tile(R, x + 1, y) - tile(R, x - 1, y),
        tile(R, x, y + 1) - tile(R, x, y - 1),
        rp - rm,
    )
    speed = [tile(V, x, y, i) for i in range(3)]
    for i in range(3):
        zm, zp = turn(speed[i])
        plus = (tile(V, x + 1, y, i), tile(V, x, y + 1, i), zp)
        minus = (tile(V, x - 1, y, i), tile(V, x, y - 1, i), zm)
        total = (plus[0] + minus[0]) + (plus[1] + minus[1]) + (plus[2] + minus[2])
        conv = (
            speed[0] * (plus[0] - minus[0])
            + speed[1] * (plus[1] - minus[1])
            + speed[2] * (plus[2] - minus[2])
        )
        pred = (1.0 - 6.0 * DT * VISC) * speed[i] + (
            DT * VISC * total - 0.5 * DT * (conv + grads[i])
        )
        mean = total * (1.0 / 6.0)
        VS[i, x - RIM, pl.ds(y - LEFT, 8), :] = jnp.where(
            kinds == 1, mean, jnp.where(kinds == 2, 0.0, pred)
        )


def advected(L, V, x, y):
    c = tile(L, x, y)
    zm, zp = turn(c)
    v = [tile(V, x, y, i) for i in range(3)]
    flux = None
    for u, m, p in (
        (v[0], tile(L, x - 1, y), tile(L, x + 1, y)),
        (v[1], tile(L, x, y - 1), tile(L, x, y + 1)),
        (v[2], zm, zp),
    ):
        term = u * jnp.where(u > 0, c - m, p - c)
        flux = term if flux is None else flux + term
    return c - DT_SET * flux


def scaled_sign(psi):
    return (TAU * psi) * lax.rsqrt(psi * psi + 1.0)


def advect(L, V, A, S, x, y):
    psi = advected(L, V, x, y)
    A[x, pl.ds(y, 8), :] = psi
    S[x, pl.ds(y, 8), :] = scaled_sign(psi)


def evolved(ref, S, x, y):
    c = tile(ref, x, y)
    s = tile(S, x, y)
    zm, zp = turn(c)
    up = s > 0
    g = None
    for m, p in (
        (tile(ref, x - 1, y), tile(ref, x + 1, y)),
        (tile(ref, x, y - 1), tile(ref, x, y + 1)),
        (zm, zp),
    ):
        low = c - jnp.minimum(jnp.minimum(m, p), c)
        high = jnp.maximum(jnp.maximum(m, p), c) - c
        d = jnp.where(up, low, high)
        g = d * d if g is None else g + d * d
    return c - s * (g * lax.rsqrt(g + 1e-30) - 1.0)


def evolve(source, target, S, x, y):
    target[x, pl.ds(y, 8), :] = evolved(source, S, x, y)


def finish(source, S, L, M, F, size_y, x, y):
    new = evolved(source, S, x, y)
    y0 = max(y, LEFT)
    y1 = min(y + 8, LEFT + size_y)
    wide = size_y // BS
    first = (y0 - LEFT) // BS
    last = (y1 - 1 - LEFT) // BS
    mark = M[(x - RIM) // BS * wide + first]
    if first != last:
        edge = LEFT + last * BS - y
        rows = lax.broadcasted_iota(jnp.int32, mark.shape, 0)
        mark = jnp.where(rows < edge, mark, M[(x - RIM) // BS * wide + last])
    value = jnp.where(mark > 0.5, new, tile(L, x, y))
    F[x - RIM, pl.ds(y0 - LEFT, y1 - y0), :] = value[y0 - y : y1 - y]


def inner_kernel(
    V, L, press, overset, count, band_ids, _, R, K, VS, A, S, B, C, F, M, ids, sems
):
    size_x, size_y, size_z = F.shape
    middle = size_y - 16
    named = copies_of([(band_ids, ids)], sems)
    later = copies_of(
        [
            (press.at[:, pl.ds(8, middle)], R.at[pl.ds(RIM, size_x), pl.ds(LEFT + 8, middle)]),
            (overset, K),
        ],
        sems,
        1,
    )
    start_all(named + later)
    core = [LEFT + y for y in range(0, size_y, 8)]
    mid = [LEFT + y for y in range(RIM, size_y - RIM, 8)]
    low, high = RIM, RIM + size_x
    sweep(low + 1, high - 1, core, functools.partial(advect, L, V, A, S))
    sweep(low + 2, high - 2, core, functools.partial(evolve, A, B, S))
    sweep(low + 3, high - 3, core, functools.partial(evolve, B, C, S))

    wait_all(named)
    wide = size_y // BS
    deep = size_z // BS
    lane = lax.broadcasted_iota(jnp.int32, (8, size_z), 1) // BS
    marks = [jnp.zeros((8, size_z), jnp.bool_) for _ in range(size_x // BS * wide)]
    held = count[0, 0]
    for s in range(MAXB):
        block = jnp.where(s < held, ids[0, 0, s], -1)
        marks = [m | (lane == block - k * deep) for k, m in enumerate(marks)]
    for k, m in enumerate(marks):
        M[k] = m.astype(F32)

    sweep(low + 4, high - 4, mid, functools.partial(finish, C, S, L, M, F, size_y))
    wait_all(later)
    sweep(low + 1, high - 1, core[1:-1], functools.partial(predict, V, R, K, VS))


def side_kernel(K, M, q_lo, q_hi, *refs):
    V, L, R, VS, A, S, B, C, F, sems = refs[9:]
    size_x, size_y = F.shape[:2]
    low, high = RIM, RIM + size_x

    def spread(x, y):
        row = 8 * (x - RIM + 1)
        for side, q in enumerate((q_lo, q_hi)):
            fill(L, V, x, side, q, (), row, size_y)
            place = LEFT + size_y if side else LEFT - 1
            R[x, pl.ds(place, 1), :] = q[pl.ds(row + 7, 1), :]

    sweep(low, high, [0], spread, 16)
    for side, q in enumerate((q_lo, q_hi)):
        place = LEFT + size_y + 2 if side else LEFT - 3
        for x, near, more in ((low, low + 1, 0), (high - 1, high - 2, 8 * (size_x + 1))):
            fill_raw(L, V, x, side, q, (), 8 * (x - RIM + 1), more, size_y)
            L[near, pl.ds(place, 1), :] = q[pl.ds(more, 1), :]

    outer = [LEFT - RIM, LEFT + size_y - RIM]
    sweep(low + 1, high - 1, outer, functools.partial(advect, L, V, A, S))

    def take(x, y):
        for side, q in enumerate((q_lo, q_hi)):
            psi = q[pl.ds(8 * (x - RIM + 1) + 2, 2), :]
            place = pl.ds(LEFT + size_y + 1 if side else LEFT - 3, 2)
            A[x, place, :] = psi
            S[x, place, :] = scaled_sign(psi)

    sweep(low + 1, high - 1, [0], take, 16)
    sweep(low + 2, high - 2, outer, functools.partial(evolve, A, B, S))
    sweep(low + 3, high - 3, outer, functools.partial(evolve, B, C, S))
    sweep(low + 4, high - 4, outer, functools.partial(finish, C, S, L, M, F, size_y))
    ends = [LEFT, LEFT + size_y - 8]
    sweep(low + 1, high - 1, ends, functools.partial(predict, V, R, K, VS))


def last_kernel(K, M, x_in, x_out, *refs):
    V, L, R, VS, A, S, B, C, F, star, new, sems = refs[9:]
    size_x, size_y = F.shape[:2]
    body = pl.ds(LEFT, size_y)
    low, high = RIM, RIM + size_x
    odd = odd_brick()
    pairs = []
    for x, upper in ((x_in, 1 - odd), (x_out, odd)):
        place = upper * high + (1 - upper) * (low - RIM)
        pairs.append((x.at[pl.ds(0, RIM)], L.at[pl.ds(place, RIM), body]))
        place = upper * high + (1 - upper) * (low - DEEP)
        for i in range(3):
            pairs.append(
                (x.at[pl.ds(RIM + i * DEEP, DEEP)], V.at[i, pl.ds(place, DEEP), body])
            )
        place = upper * high + (1 - upper) * (low - 1)
        pairs.append((x.at[pl.ds(SLABS - 1, 1)], R.at[pl.ds(place, 1), body]))
    middle = pl.ds(1, size_x - 2)
    pairs.append((VS.at[:, middle], star.at[:, middle]))
    middle = pl.ds(RIM, size_x - 2 * RIM)
    pairs.append((F.at[middle], new.at[middle]))
    copies = copies_of(pairs, sems)
    start_all(copies)
    wait_all(copies[:-2])
    for x, upper in ((x_in, 1 - odd), (x_out, odd)):
        place = upper * high + (1 - upper) * (low - DEEP)
        edge = upper * high + (1 - upper) * (low - 1)
        first = upper * 8
        for side in range(2):
            lead = (SLABS + side,)
            for k in range(DEEP):
                fill(L, V, place + k, side, x, lead, first + k * 8, size_y)
            fill_raw(L, V, edge, side, x, lead, 16 - upper * 8, 24 - upper * 24, size_y)

    for x in (low, high - 1):
        for y in range(LEFT, LEFT + size_y, 8):
            predict(V, R, K, VS, x, y)
    late = copies_of(
        [(VS.at[:, pl.ds(x, 1)], star.at[:, pl.ds(x, 1)]) for x in (0, size_x - 1)],
        sems,
        len(copies),
    )
    start_all(late)
    tiles = range(LEFT - RIM, LEFT + size_y, 8)

    def ends(depth, cell):
        for k in range(4):
            for x in (low - depth + k, high + depth - 1 - k):
                for y in tiles:
                    cell(x, y)

    ends(3, functools.partial(advect, L, V, A, S))
    ends(2, functools.partial(evolve, A, B, S))
    ends(1, functools.partial(evolve, B, C, S))
    ends(0, functools.partial(finish, C, S, L, M, F, size_y))
    tail = copies_of(
        [(F.at[pl.ds(x, RIM)], new.at[pl.ds(x, RIM)]) for x in (0, size_x - RIM)],
        sems,
        len(copies) + len(late),
    )
    start_all(tail)
    wait_all(copies[-2:] + late + tail)


def moved(array, axis, step):
    peers = lax.axis_size(axis)
    return lax.ppermute(array, axis, [(i, (i + step) % peers) for i in range(peers)])


def swapped(array, axis, shift):
    peers = lax.axis_size(axis)
    pairs = [(i, (((i + shift) ^ 1) - shift) % peers) for i in range(peers)]
    return lax.ppermute(array, axis, pairs)


def shards(velocity, pressure, level_set, overset, band_count, band_ids):
    size_x, size_y, size_z = level_set.shape
    plain = level_set.shape
    padded = (size_x + 2 * RIM, LEFT + size_y + 8, size_z)
    x_face = (SLABS + 2, size_y, size_z)
    y_face = ((size_x + 2) * 8, size_z)
    marks = (size_x // BS * (size_y // BS), 8, size_z)

    y_low, y_high, V, L, R = call(
        pack_kernel,
        [("hbm", velocity), ("hbm", pressure), ("hbm", level_set)],
        [("vmem", y_face, F32)] * 2
        + [("vmem", (3,) + padded, F32), ("vmem", padded, F32), ("vmem", padded, F32)],
        "pack",
        sems=8,
    )
    q_lo = moved(y_high, "col", 1)
    q_hi = moved(y_low, "col", -1)
    R, K, VS, A, S, B, C, F, M = call(
        inner_kernel,
        [("vmem", V), ("vmem", L), ("hbm", pressure), ("hbm", overset)]
        + [("smem", band_count), ("hbm", band_ids), ("vmem", R)],
        [("vmem", padded, F32), ("vmem", plain, jnp.int32), ("vmem", (3,) + plain, F32)]
        + [("vmem", padded, F32)] * 4
        + [("vmem", plain, F32), ("vmem", marks, F32)],
        "inner",
        aliases={6: 0},
        scratch=[pltpu.SMEM(band_ids.shape, jnp.int32)],
        sems=3,
        flops=60 << 20,
    )
    x_in, x_out = call(
        relay_kernel,
        [("vmem", a) for a in (V, L, R, M, q_lo, q_hi)],
        [("vmem", x_face, F32)] * 2,
        "relay",
        sems=14,
    )
    x_in = swapped(x_in, "brick", 0)
    x_out = swapped(x_out, "brick", 1)
    state = [V, L, R, VS, A, S, B, C, F]
    held = [("vmem", a) for a in (K, M, q_lo, q_hi)]
    state = call(
        side_kernel,
        held + [("vmem", a) for a in state],
        [("vmem", a.shape, F32) for a in state],
        "side",
        aliases={len(held) + i: i for i in range(len(state))},
        flops=60 << 20,
        sems=1,
    )
    held = [("vmem", a) for a in (K, M, x_in, x_out)]
    *_, velocity_star, level_set_new = call(
        last_kernel,
        held + [("vmem", a) for a in state],
        [("vmem", a.shape, F32) for a in state]
        + [("hbm", velocity.shape, F32), ("hbm", plain, F32)],
        "last",
        aliases={len(held) + i: i for i in range(len(state))},
        sems=16,
    )
    return (velocity_star, level_set_new)


def solution(mesh):
    return jax.shard_map(
        shards,
        mesh=mesh,
        in_specs=(
            P(None, "brick", "col", None),
            P("brick", "col", None),
            P("brick", "col", None),
            P("brick", "col", None),
            P("brick", "col"),
            P("brick", "col", None),
        ),
        out_specs=(P(None, "brick", "col", None), P("brick", "col", None)),
        check_vma=False,
    )
```

```python
import functools

import jax
import jax.numpy as jnp
from jax import lax
from jax.experimental import pallas as pl
from jax.experimental.pallas import tpu as pltpu
from jax.sharding import PartitionSpec as P

BS = 16
REINIT = 3
MAXB = 16
RIM = 4
DEEP = 3
SLABS = RIM + 3 * DEEP + 1
CORNER = 32
LEFT = 8
UNROLL = 80

DT = 0.1
VISC = 0.5
DT_SET = 0.2
TAU = 0.5

F32 = jnp.float32
ANY = pl.BlockSpec(memory_space=pl.ANY)
VM = pl.BlockSpec(memory_space=pltpu.VMEM)
SM = pl.BlockSpec(memory_space=pltpu.SMEM)


def call(kernel, args, outs, name, aliases=None, sems=0, flops=1 << 20, scratch=()):
    specs = {"vmem": VM, "hbm": ANY, "smem": SM}
    spaces = {"vmem": pltpu.VMEM, "hbm": pltpu.HBM}
    operands = [
        pltpu.with_memory_space_constraint(a, spaces[k]) if k in spaces else a for k, a in args
    ]
    shapes = [
        pltpu.VMEM(s, t) if k == "vmem" else jax.ShapeDtypeStruct(s, t) for k, s, t in outs
    ]
    return pl.pallas_call(
        kernel,
        out_shape=shapes,
        in_specs=[specs[k] for k, _ in args],
        out_specs=[specs[k] for k, _, _ in outs],
        input_output_aliases=aliases or {},
        scratch_shapes=list(scratch) + [pltpu.SemaphoreType.DMA((sems,))],
        cost_estimate=pl.CostEstimate(
            flops=flops, bytes_accessed=4 << 20, transcendentals=0
        ),
        compiler_params=pltpu.CompilerParams(vmem_limit_bytes=8 << 20),
        name=name,
    )(*operands)


def copies_of(pairs, sems, first=0):
    return [
        pltpu.make_async_copy(s, d, sems.at[first + i]) for i, (s, d) in enumerate(pairs)
    ]


def start_all(copies):
    for copy in copies:
        copy.start()


def wait_all(copies):
    for copy in copies:
        copy.wait()


def sweep(low, high, tiles, cell, limit=UNROLL):
    rows = high - low
    group = max(g for g in range(1, rows + 1) if rows % g == 0 and g * len(tiles) <= limit)

    def some(i, carry):
        for k in range(group):
            for y in tiles:
                cell(low + i * group + k, y)
        return carry

    if group == rows:
        some(0, 0)
    else:
        lax.fori_loop(0, rows // group, some, 0)


def odd_brick():
    return lax.axis_index("brick") % 2


def pack_kernel(vel, press, level, x_in, x_out, y_lo, y_hi, V, L, R, sems):
    size_x, size_y = level.shape[:2]
    odd = odd_brick()
    inner = pl.ds(RIM, size_x)

    def part(first, count):
        rows, place = pl.ds(first, count), pl.ds(LEFT + first, count)
        return [
            (level.at[:, rows], L.at[inner, place]),
            (vel.at[:, :, rows], V.at[:, inner, place]),
            (press.at[:, rows], R.at[inner, place]),
        ]

    strips = part(0, 8) + part(size_y - 8, 8)
    rest = []
    for out, high in ((x_in, 1 - odd), (x_out, odd)):
        def rows(n):
            return pl.ds(high * (size_x - n), n)

        rest.append((level.at[rows(RIM)], out.at[pl.ds(0, RIM)]))
        for i in range(3):
            rest.append((vel.at[i, rows(DEEP)], out.at[pl.ds(RIM + i * DEEP, DEEP)]))
        rest.append((press.at[rows(1)], out.at[pl.ds(RIM + 3 * DEEP, 1)]))
    rest += part(8, size_y - 16)[:2]
    strips = copies_of(strips, sems)
    rest = copies_of(rest, sems, len(strips))
    start_all(strips + rest)

    def put(out, row, ref, x, y, n, *lead):
        out[pl.ds(row, n), :] = ref[(*lead, x, pl.ds(LEFT + y, n), slice(None))]

    def gather(out, high, x, y):
        row = 8 * (x - RIM + 1)
        near = size_y - 1 if high else 0
        put(out, row, L, x, size_y - 2 if high else 0, 2)
        first = size_y - 7 if high else -1
        psi = advected(L, V, x, LEFT + first)
        place = (size_y - 3 if high else 1) - first
        out[pl.ds(row + 2, 2), :] = psi[place : place + 2]
        for i in range(3):
            put(out, row + 4 + i, V, x, near, 1, i)
        put(out, row + 7, R, x, near, 1)

    for high, out in enumerate((y_lo, y_hi)):
        wait_all(strips[3 * high : 3 * high + 3])
        sweep(RIM, RIM + size_x, [0], functools.partial(gather, out, high), 16)
        for x, near, more in (
            (RIM, RIM + 1, 0),
            (RIM + size_x - 1, RIM + size_x - 2, 8 * (size_x + 1)),
        ):
            put(out, 8 * (x - RIM + 1) + 2, L, x, size_y - 4 if high else 2, 2)
            put(out, more, L, near, size_y - 3 if high else 2, 1)
            for i in range(3):
                put(out, more + 1 + 2 * i, V, x, size_y - 3 if high else 1, 2, i)
    wait_all(rest)


def fill(L, V, x, side, ref, lead, row, size_y):
    place = LEFT + size_y if side else LEFT - 2
    L[x, pl.ds(place, 2), :] = ref[(*lead, pl.ds(row, 2), slice(None))]
    place = LEFT + size_y if side else LEFT - 1
    for i in range(3):
        V[i, x, pl.ds(place, 1), :] = ref[(*lead, pl.ds(row + 4 + i, 1), slice(None))]


def fill_raw(L, V, x, side, ref, lead, row, more, size_y):
    place = LEFT + size_y + 2 if side else LEFT - 4
    L[x, pl.ds(place, 2), :] = ref[(*lead, pl.ds(row + 2, 2), slice(None))]
    place = LEFT + size_y + 1 if side else LEFT - 3
    for i in range(3):
        V[i, x, pl.ds(place, 2), :] = ref[(*lead, pl.ds(more + 1 + 2 * i, 2), slice(None))]


def relay_kernel(after, q_lo, q_hi, z_in, z_out, sems):
    rows = q_lo.shape[0]
    odd = odd_brick()
    pairs = []
    for out, high in ((z_in, 1 - odd), (z_out, odd)):
        start = pl.multiple_of(high * (rows - CORNER), 8)
        for side, q in enumerate((q_lo, q_hi)):
            pairs.append((q.at[pl.ds(start, CORNER)], out.at[side]))
    copies = copies_of(pairs, sems)
    start_all(copies)
    wait_all(copies)


def turn(value):
    return pltpu.roll(value, 1, 1), pltpu.roll(value, value.shape[1] - 1, 1)


def tile(ref, x, y, *lead):
    return ref[(*lead, x, pl.ds(y, 8), slice(None))]


def predict(V, R, K, VS, x, y):
    kinds = tile(K, x - RIM, y - LEFT)
    rm, rp = turn(tile(R, x, y))
    grads = (
        tile(R, x + 1, y) - tile(R, x - 1, y),
        tile(R, x, y + 1) - tile(R, x, y - 1),
        rp - rm,
    )
    speed = [tile(V, x, y, i) for i in range(3)]
    for i in range(3):
        zm, zp = turn(speed[i])
        plus = (tile(V, x + 1, y, i), tile(V, x, y + 1, i), zp)
        minus = (tile(V, x - 1, y, i), tile(V, x, y - 1, i), zm)
        total = (plus[0] + minus[0]) + (plus[1] + minus[1]) + (plus[2] + minus[2])
        conv = (
            speed[0] * (plus[0] - minus[0])
            + speed[1] * (plus[1] - minus[1])
            + speed[2] * (plus[2] - minus[2])
        )
        pred = (1.0 - 6.0 * DT * VISC) * speed[i] + (
            DT * VISC * total - 0.5 * DT * (conv + grads[i])
        )
        mean = total * (1.0 / 6.0)
        VS[i, x - RIM, pl.ds(y - LEFT, 8), :] = jnp.where(
            kinds == 1, mean, jnp.where(kinds == 2, 0.0, pred)
        )


def advected(L, V, x, y):
    c = tile(L, x, y)
    zm, zp = turn(c)
    v = [tile(V, x, y, i) for i in range(3)]
    flux = None
    for u, m, p in (
        (v[0], tile(L, x - 1, y), tile(L, x + 1, y)),
        (v[1], tile(L, x, y - 1), tile(L, x, y + 1)),
        (v[2], zm, zp),
    ):
        term = u * jnp.where(u > 0, c - m, p - c)
        flux = term if flux is None else flux + term
    return c - DT_SET * flux


def scaled_sign(psi):
    return (TAU * psi) * lax.rsqrt(psi * psi + 1.0)


def advect(L, V, A, S, x, y):
    psi = advected(L, V, x, y)
    A[x, pl.ds(y, 8), :] = psi
    S[x, pl.ds(y, 8), :] = scaled_sign(psi)


def evolved(ref, S, x, y):
    c = tile(ref, x, y)
    s = tile(S, x, y)
    zm, zp = turn(c)
    up = s > 0
    g = None
    for m, p in (
        (tile(ref, x - 1, y), tile(ref, x + 1, y)),
        (tile(ref, x, y - 1), tile(ref, x, y + 1)),
        (zm, zp),
    ):
        low = c - jnp.minimum(jnp.minimum(m, p), c)
        high = jnp.maximum(jnp.maximum(m, p), c) - c
        d = jnp.where(up, low, high)
        g = d * d if g is None else g + d * d
    return c - s * (g * lax.rsqrt(g + 1e-30) - 1.0)


def evolve(source, target, S, x, y):
    target[x, pl.ds(y, 8), :] = evolved(source, S, x, y)


def finish(source, S, L, M, F, size_y, x, y):
    new = evolved(source, S, x, y)
    y0 = max(y, LEFT)
    y1 = min(y + 8, LEFT + size_y)
    wide = size_y // BS
    first = (y0 - LEFT) // BS
    last = (y1 - 1 - LEFT) // BS
    mark = M[(x - RIM) // BS * wide + first]
    if first != last:
        edge = LEFT + last * BS - y
        rows = lax.broadcasted_iota(jnp.int32, mark.shape, 0)
        mark = jnp.where(rows < edge, mark, M[(x - RIM) // BS * wide + last])
    value = jnp.where(mark > 0.5, new, tile(L, x, y))
    F[x - RIM, pl.ds(y0 - LEFT, y1 - y0), :] = value[y0 - y : y1 - y]


def inner_kernel(
    V, L, press, overset, count, band_ids, _, R, K, VS, A, S, B, C, F, M, ids, sems
):
    size_x, size_y, size_z = F.shape
    middle = size_y - 16
    named = copies_of([(band_ids, ids)], sems)
    later = copies_of(
        [
            (press.at[:, pl.ds(8, middle)], R.at[pl.ds(RIM, size_x), pl.ds(LEFT + 8, middle)]),
            (overset, K),
        ],
        sems,
        1,
    )
    start_all(named + later)
    core = [LEFT + y for y in range(0, size_y, 8)]
    mid = [LEFT + y for y in range(RIM, size_y - RIM, 8)]
    low, high = RIM, RIM + size_x
    sweep(low + 1, high - 1, core, functools.partial(advect, L, V, A, S))
    sweep(low + 2, high - 2, core, functools.partial(evolve, A, B, S))
    sweep(low + 3, high - 3, core, functools.partial(evolve, B, C, S))

    wait_all(named)
    wide = size_y // BS
    deep = size_z // BS
    lane = lax.broadcasted_iota(jnp.int32, (8, size_z), 1) // BS
    marks = [jnp.zeros((8, size_z), jnp.bool_) for _ in range(size_x // BS * wide)]
    held = count[0, 0]
    for s in range(MAXB):
        block = jnp.where(s < held, ids[0, 0, s], -1)
        marks = [m | (lane == block - k * deep) for k, m in enumerate(marks)]
    for k, m in enumerate(marks):
        M[k] = m.astype(F32)

    sweep(low + 4, high - 4, mid, functools.partial(finish, C, S, L, M, F, size_y))
    wait_all(later)
    sweep(low + 1, high - 1, core[1:-1], functools.partial(predict, V, R, K, VS))


def edge_kernel(
    K, M, x_in, x_out, q_lo, q_hi, *refs
):
    V, L, R, VS, A, S, B, C, F, star, sems = refs[9:]
    size_x, size_y = F.shape[:2]
    body = pl.ds(LEFT, size_y)
    low, high = RIM, RIM + size_x
    odd = odd_brick()
    pairs = []
    for x, upper in ((x_in, 1 - odd), (x_out, odd)):
        place = upper * high + (1 - upper) * (low - RIM)
        pairs.append((x.at[pl.ds(0, RIM)], L.at[pl.ds(place, RIM), body]))
        place = upper * high + (1 - upper) * (low - DEEP)
        for i in range(3):
            pairs.append(
                (x.at[pl.ds(RIM + i * DEEP, DEEP)], V.at[i, pl.ds(place, DEEP), body])
            )
        place = upper * high + (1 - upper) * (low - 1)
        pairs.append((x.at[pl.ds(RIM + 3 * DEEP, 1)], R.at[pl.ds(place, 1), body]))
    copies = copies_of(pairs, sems)
    start_all(copies)

    def spread(x, y):
        row = 8 * (x - RIM + 1)
        for side, q in enumerate((q_lo, q_hi)):
            fill(L, V, x, side, q, (), row, size_y)
            place = LEFT + size_y if side else LEFT - 1
            R[x, pl.ds(place, 1), :] = q[pl.ds(row + 7, 1), :]

    sweep(low, high, [0], spread, 16)
    for side, q in enumerate((q_lo, q_hi)):
        place = LEFT + size_y + 2 if side else LEFT - 3
        for x, near, more in ((low, low + 1, 0), (high - 1, high - 2, 8 * (size_x + 1))):
            fill_raw(L, V, x, side, q, (), 8 * (x - RIM + 1), more, size_y)
            L[near, pl.ds(place, 1), :] = q[pl.ds(more, 1), :]
    wait_all(copies)

    core = [LEFT + y for y in range(0, size_y, 8)]
    mid = [LEFT + y for y in range(RIM, size_y - RIM, 8)]
    outer = [LEFT - RIM, LEFT + size_y - RIM]
    step = functools.partial(predict, V, R, K, VS)
    sweep(low + 1, high - 1, [core[0], core[-1]], step)
    for x in (low, high - 1):
        for y in core:
            step(x, y)
    out = copies_of([(VS.at[i], star.at[i]) for i in range(3)], sems, len(copies))
    start_all(out)

    def ring(depth, cell):
        sweep(low - depth, high + depth, outer, cell)
        sweep(low - depth, low - depth + 4, mid, cell)
        sweep(high + depth - 4, high + depth, mid, cell)

    ring(3, functools.partial(advect, L, V, A, S))

    def take(x, y):
        for side, q in enumerate((q_lo, q_hi)):
            psi = q[pl.ds(8 * (x - RIM + 1) + 2, 2), :]
            place = pl.ds(LEFT + size_y + 1 if side else LEFT - 3, 2)
            A[x, place, :] = psi
            S[x, place, :] = scaled_sign(psi)

    sweep(low + 1, high - 1, [0], take, 16)
    ring(2, functools.partial(evolve, A, B, S))
    ring(1, functools.partial(evolve, B, C, S))
    ring(0, functools.partial(finish, C, S, L, M, F, size_y))
    wait_all(out)


def corner_kernel(M, z_in, z_out, *refs):
    V, L, A, S, B, C, F, new, sems = refs[7:]
    size_x, size_y = F.shape[:2]
    low, high = RIM, RIM + size_x
    early = copies_of(
        [(F.at[pl.ds(3, size_x - 6)], new.at[pl.ds(3, size_x - 6)])], sems
    )
    start_all(early)
    odd = odd_brick()
    for z, upper in ((z_in, 1 - odd), (z_out, odd)):
        place = upper * high + (1 - upper) * (low - DEEP)
        edge = upper * high + (1 - upper) * (low - 1)
        first = upper * 8
        for side in range(2):
            for k in range(DEEP):
                fill(L, V, place + k, side, z, (side,), first + k * 8, size_y)
            fill_raw(
                L, V, edge, side, z, (side,), 16 - upper * 8, 24 - upper * 24, size_y
            )

    outer = [LEFT - RIM, LEFT + size_y - RIM]

    def ends(depth, cell):
        rows = 4 if depth else 3
        for k in range(rows):
            for x in (low - depth + k, high + depth - 1 - k):
                for y in outer:
                    cell(x, y)

    ends(3, functools.partial(advect, L, V, A, S))
    ends(2, functools.partial(evolve, A, B, S))
    ends(1, functools.partial(evolve, B, C, S))
    ends(0, functools.partial(finish, C, S, L, M, F, size_y))
    late = copies_of(
        [(F.at[pl.ds(x, 3)], new.at[pl.ds(x, 3)]) for x in (0, size_x - 3)], sems, 1
    )
    start_all(late)
    wait_all(early + late)


def moved(array, axis, step):
    peers = lax.axis_size(axis)
    return lax.ppermute(array, axis, [(i, (i + step) % peers) for i in range(peers)])


def swapped(array, axis, shift):
    peers = lax.axis_size(axis)
    pairs = [(i, (((i + shift) ^ 1) - shift) % peers) for i in range(peers)]
    return lax.ppermute(array, axis, pairs)


def shards(velocity, pressure, level_set, overset, band_count, band_ids):
    size_x, size_y, size_z = level_set.shape
    plain = level_set.shape
    padded = (size_x + 2 * RIM, LEFT + size_y + 8, size_z)
    x_face = (SLABS, size_y, size_z)
    y_face = ((size_x + 2) * 8, size_z)
    marks = (size_x // BS * (size_y // BS), 8, size_z)

    x_in, x_out, y_low, y_high, V, L, R = call(
        pack_kernel,
        [("hbm", velocity), ("hbm", pressure), ("hbm", level_set)],
        [("vmem", x_face, F32)] * 2
        + [("vmem", y_face, F32)] * 2
        + [("vmem", (3,) + padded, F32), ("vmem", padded, F32), ("vmem", padded, F32)],
        "pack",
        sems=24,
    )
    q_lo = moved(y_high, "col", 1)
    q_hi = moved(y_low, "col", -1)
    x_in = swapped(x_in, "brick", 0)
    x_out = swapped(x_out, "brick", 1)
    R, K, VS, A, S, B, C, F, M = call(
        inner_kernel,
        [("vmem", V), ("vmem", L), ("hbm", pressure), ("hbm", overset)]
        + [("smem", band_count), ("hbm", band_ids), ("vmem", R)],
        [("vmem", padded, F32), ("vmem", plain, jnp.int32), ("vmem", (3,) + plain, F32)]
        + [("vmem", padded, F32)] * 4
        + [("vmem", plain, F32), ("vmem", marks, F32)],
        "inner",
        aliases={6: 0},
        scratch=[pltpu.SMEM(band_ids.shape, jnp.int32)],
        sems=3,
        flops=60 << 26,
    )
    z_in, z_out = call(
        relay_kernel,
        [("vmem", M), ("vmem", q_lo), ("vmem", q_hi)],
        [("vmem", (2, CORNER, size_z), F32)] * 2,
        "relay",
        sems=4,
    )
    z_in = swapped(z_in, "brick", 0)
    z_out = swapped(z_out, "brick", 1)
    state = [V, L, R, VS, A, S, B, C, F]
    held = [("vmem", K), ("vmem", M)] + [("vmem", a) for a in (x_in, x_out, q_lo, q_hi)]
    *state, velocity_star = call(
        edge_kernel,
        held + [("vmem", a) for a in state],
        [("vmem", a.shape, F32) for a in state] + [("hbm", velocity.shape, F32)],
        "edge",
        aliases={len(held) + i: i for i in range(len(state))},
        sems=13,
        flops=60 << 26,
    )
    V, L, R, VS, A, S, B, C, F = state
    state = [V, L, A, S, B, C, F]
    held = [("vmem", M), ("vmem", z_in), ("vmem", z_out)]
    *state, level_set_new = call(
        corner_kernel,
        held + [("vmem", a) for a in state],
        [("vmem", a.shape, F32) for a in state] + [("hbm", plain, F32)],
        "corner",
        aliases={len(held) + i: i for i in range(len(state))},
        sems=3,
    )
    return (velocity_star, level_set_new)


def solution(mesh):
    return jax.shard_map(
        shards,
        mesh=mesh,
        in_specs=(
            P(None, "brick", "col", None),
            P("brick", "col", None),
            P("brick", "col", None),
            P("brick", "col", None),
            P("brick", "col"),
            P("brick", "col", None),
        ),
        out_specs=(P(None, "brick", "col", None), P("brick", "col", None)),
        check_vma=False,
    )
```

```python
import functools

import jax
import jax.numpy as jnp
from jax import lax
from jax.experimental import pallas as pl
from jax.experimental.pallas import tpu as pltpu
from jax.sharding import PartitionSpec as P

BS = 16
REINIT = 3
MAXB = 16
RIM = 4
DEEP = 3
SLABS = RIM + 3 * DEEP + 1
CORNER = 32
LEFT = 8
UNROLL = 120

DT = 0.1
VISC = 0.5
DT_SET = 0.2
TAU = 0.5

F32 = jnp.float32
ANY = pl.BlockSpec(memory_space=pl.ANY)
VM = pl.BlockSpec(memory_space=pltpu.VMEM)
SM = pl.BlockSpec(memory_space=pltpu.SMEM)


def call(kernel, args, outs, name, aliases=None, sems=0, flops=1 << 20, scratch=()):
    specs = {"vmem": VM, "hbm": ANY, "smem": SM}
    spaces = {"vmem": pltpu.VMEM, "hbm": pltpu.HBM}
    operands = [
        pltpu.with_memory_space_constraint(a, spaces[k]) if k in spaces else a for k, a in args
    ]
    shapes = [
        pltpu.VMEM(s, t) if k == "vmem" else jax.ShapeDtypeStruct(s, t) for k, s, t in outs
    ]
    return pl.pallas_call(
        kernel,
        out_shape=shapes,
        in_specs=[specs[k] for k, _ in args],
        out_specs=[specs[k] for k, _, _ in outs],
        input_output_aliases=aliases or {},
        scratch_shapes=list(scratch) + [pltpu.SemaphoreType.DMA((sems,))],
        cost_estimate=pl.CostEstimate(
            flops=flops, bytes_accessed=4 << 20, transcendentals=0
        ),
        compiler_params=pltpu.CompilerParams(vmem_limit_bytes=8 << 20),
        name=name,
    )(*operands)


def copies_of(pairs, sems, first=0):
    return [
        pltpu.make_async_copy(s, d, sems.at[first + i]) for i, (s, d) in enumerate(pairs)
    ]


def start_all(copies):
    for copy in copies:
        copy.start()


def wait_all(copies):
    for copy in copies:
        copy.wait()


def sweep(low, high, tiles, cell, limit=UNROLL):
    rows = high - low
    group = max(g for g in range(1, rows + 1) if rows % g == 0 and g * len(tiles) <= limit)

    def some(i, carry):
        for k in range(group):
            for y in tiles:
                cell(low + i * group + k, y)
        return carry

    if group == rows:
        some(0, 0)
    else:
        lax.fori_loop(0, rows // group, some, 0)


def odd_brick():
    return lax.axis_index("brick") % 2


def pack_kernel(vel, press, level, x_in, x_out, y_lo, y_hi, V, L, R, sems):
    size_x, size_y = level.shape[:2]
    odd = odd_brick()
    inner = pl.ds(RIM, size_x)

    def part(first, count):
        rows, place = pl.ds(first, count), pl.ds(LEFT + first, count)
        return [
            (level.at[:, rows], L.at[inner, place]),
            (vel.at[:, :, rows], V.at[:, inner, place]),
            (press.at[:, rows], R.at[inner, place]),
        ]

    strips = part(0, 8) + part(size_y - 8, 8)
    rest = []
    for out, high in ((x_in, 1 - odd), (x_out, odd)):
        def rows(n):
            return pl.ds(high * (size_x - n), n)

        rest.append((level.at[rows(RIM)], out.at[pl.ds(0, RIM)]))
        for i in range(3):
            rest.append((vel.at[i, rows(DEEP)], out.at[pl.ds(RIM + i * DEEP, DEEP)]))
        rest.append((press.at[rows(1)], out.at[pl.ds(RIM + 3 * DEEP, 1)]))
    rest += part(8, size_y - 16)[:2]
    strips = copies_of(strips, sems)
    rest = copies_of(rest, sems, len(strips))
    start_all(strips + rest)

    def put(out, row, ref, x, y, n, *lead):
        out[pl.ds(row, n), :] = ref[(*lead, x, pl.ds(LEFT + y, n), slice(None))]

    def gather(out, high, x, y):
        row = 8 * (x - RIM + 1)
        near = size_y - 1 if high else 0
        put(out, row, L, x, size_y - 2 if high else 0, 2)
        first = size_y - 7 if high else -1
        psi = advected(L, V, x, LEFT + first)
        place = (size_y - 3 if high else 1) - first
        out[pl.ds(row + 2, 2), :] = psi[place : place + 2]
        for i in range(3):
            put(out, row + 4 + i, V, x, near, 1, i)
        put(out, row + 7, R, x, near, 1)

    for high, out in enumerate((y_lo, y_hi)):
        wait_all(strips[3 * high : 3 * high + 3])
        sweep(RIM, RIM + size_x, [0], functools.partial(gather, out, high), 16)
        for x, near, more in (
            (RIM, RIM + 1, 0),
            (RIM + size_x - 1, RIM + size_x - 2, 8 * (size_x + 1)),
        ):
            put(out, 8 * (x - RIM + 1) + 2, L, x, size_y - 4 if high else 2, 2)
            put(out, more, L, near, size_y - 3 if high else 2, 1)
            for i in range(3):
                put(out, more + 1 + 2 * i, V, x, size_y - 3 if high else 1, 2, i)
    wait_all(rest)


def fill(L, V, x, side, ref, lead, row, size_y):
    place = LEFT + size_y if side else LEFT - 2
    L[x, pl.ds(place, 2), :] = ref[(*lead, pl.ds(row, 2), slice(None))]
    place = LEFT + size_y if side else LEFT - 1
    for i in range(3):
        V[i, x, pl.ds(place, 1), :] = ref[(*lead, pl.ds(row + 4 + i, 1), slice(None))]


def fill_raw(L, V, x, side, ref, lead, row, more, size_y):
    place = LEFT + size_y + 2 if side else LEFT - 4
    L[x, pl.ds(place, 2), :] = ref[(*lead, pl.ds(row + 2, 2), slice(None))]
    place = LEFT + size_y + 1 if side else LEFT - 3
    for i in range(3):
        V[i, x, pl.ds(place, 2), :] = ref[(*lead, pl.ds(more + 1 + 2 * i, 2), slice(None))]


def relay_kernel(after, q_lo, q_hi, z_in, z_out, sems):
    rows = q_lo.shape[0]
    odd = odd_brick()
    pairs = []
    for out, high in ((z_in, 1 - odd), (z_out, odd)):
        start = pl.multiple_of(high * (rows - CORNER), 8)
        for side, q in enumerate((q_lo, q_hi)):
            pairs.append((q.at[pl.ds(start, CORNER)], out.at[side]))
    copies = copies_of(pairs, sems)
    start_all(copies)
    wait_all(copies)


def turn(value):
    return pltpu.roll(value, 1, 1), pltpu.roll(value, value.shape[1] - 1, 1)


def tile(ref, x, y, *lead):
    return ref[(*lead, x, pl.ds(y, 8), slice(None))]


def predict(V, R, K, VS, x, y):
    kinds = tile(K, x - RIM, y - LEFT)
    rm, rp = turn(tile(R, x, y))
    grads = (
        tile(R, x + 1, y) - tile(R, x - 1, y),
        tile(R, x, y + 1) - tile(R, x, y - 1),
        rp - rm,
    )
    speed = [tile(V, x, y, i) for i in range(3)]
    for i in range(3):
        zm, zp = turn(speed[i])
        plus = (tile(V, x + 1, y, i), tile(V, x, y + 1, i), zp)
        minus = (tile(V, x - 1, y, i), tile(V, x, y - 1, i), zm)
        total = (plus[0] + minus[0]) + (plus[1] + minus[1]) + (plus[2] + minus[2])
        conv = (
            speed[0] * (plus[0] - minus[0])
            + speed[1] * (plus[1] - minus[1])
            + speed[2] * (plus[2] - minus[2])
        )
        pred = (1.0 - 6.0 * DT * VISC) * speed[i] + (
            DT * VISC * total - 0.5 * DT * (conv + grads[i])
        )
        mean = total * (1.0 / 6.0)
        VS[i, x - RIM, pl.ds(y - LEFT, 8), :] = jnp.where(
            kinds == 1, mean, jnp.where(kinds == 2, 0.0, pred)
        )


def advected(L, V, x, y):
    c = tile(L, x, y)
    zm, zp = turn(c)
    v = [tile(V, x, y, i) for i in range(3)]
    flux = None
    for u, m, p in (
        (v[0], tile(L, x - 1, y), tile(L, x + 1, y)),
        (v[1], tile(L, x, y - 1), tile(L, x, y + 1)),
        (v[2], zm, zp),
    ):
        term = u * jnp.where(u > 0, c - m, p - c)
        flux = term if flux is None else flux + term
    return c - DT_SET * flux


def scaled_sign(psi):
    return (TAU * psi) * lax.rsqrt(psi * psi + 1.0)


def advect(L, V, A, S, x, y):
    psi = advected(L, V, x, y)
    A[x, pl.ds(y, 8), :] = psi
    S[x, pl.ds(y, 8), :] = scaled_sign(psi)


def evolved(ref, S, x, y):
    c = tile(ref, x, y)
    s = tile(S, x, y)
    zm, zp = turn(c)
    up = s > 0
    g = None
    for m, p in (
        (tile(ref, x - 1, y), tile(ref, x + 1, y)),
        (tile(ref, x, y - 1), tile(ref, x, y + 1)),
        (zm, zp),
    ):
        low = c - jnp.minimum(jnp.minimum(m, p), c)
        high = jnp.maximum(jnp.maximum(m, p), c) - c
        d = jnp.where(up, low, high)
        g = d * d if g is None else g + d * d
    return c - s * (g * lax.rsqrt(g + 1e-30) - 1.0)


def evolve(source, target, S, x, y):
    target[x, pl.ds(y, 8), :] = evolved(source, S, x, y)


def finish(source, S, L, M, F, size_y, x, y):
    new = evolved(source, S, x, y)
    y0 = max(y, LEFT)
    y1 = min(y + 8, LEFT + size_y)
    wide = size_y // BS
    first = (y0 - LEFT) // BS
    last = (y1 - 1 - LEFT) // BS
    mark = M[(x - RIM) // BS * wide + first]
    if first != last:
        edge = LEFT + last * BS - y
        rows = lax.broadcasted_iota(jnp.int32, mark.shape, 0)
        mark = jnp.where(rows < edge, mark, M[(x - RIM) // BS * wide + last])
    value = jnp.where(mark > 0.5, new, tile(L, x, y))
    F[x - RIM, pl.ds(y0 - LEFT, y1 - y0), :] = value[y0 - y : y1 - y]


def inner_kernel(
    V, L, press, overset, count, band_ids, _, R, K, VS, A, S, B, C, F, M, ids, sems
):
    size_x, size_y, size_z = F.shape
    middle = size_y - 16
    named = copies_of([(band_ids, ids)], sems)
    later = copies_of(
        [
            (press.at[:, pl.ds(8, middle)], R.at[pl.ds(RIM, size_x), pl.ds(LEFT + 8, middle)]),
            (overset, K),
        ],
        sems,
        1,
    )
    start_all(named + later)
    core = [LEFT + y for y in range(0, size_y, 8)]
    mid = [LEFT + y for y in range(RIM, size_y - RIM, 8)]
    low, high = RIM, RIM + size_x
    sweep(low + 1, high - 1, core, functools.partial(advect, L, V, A, S))
    sweep(low + 2, high - 2, core, functools.partial(evolve, A, B, S))
    sweep(low + 3, high - 3, core, functools.partial(evolve, B, C, S))

    wait_all(named)
    wide = size_y // BS
    deep = size_z // BS
    lane = lax.broadcasted_iota(jnp.int32, (8, size_z), 1) // BS
    marks = [jnp.zeros((8, size_z), jnp.bool_) for _ in range(size_x // BS * wide)]
    held = count[0, 0]
    for s in range(MAXB):
        block = jnp.where(s < held, ids[0, 0, s], -1)
        marks = [m | (lane == block - k * deep) for k, m in enumerate(marks)]
    for k, m in enumerate(marks):
        M[k] = m.astype(F32)

    sweep(low + 4, high - 4, mid, functools.partial(finish, C, S, L, M, F, size_y))
    wait_all(later)
    sweep(low + 1, high - 1, core[1:-1], functools.partial(predict, V, R, K, VS))


def edge_kernel(
    K, M, x_in, x_out, q_lo, q_hi, *refs
):
    V, L, R, VS, A, S, B, C, F, star, sems = refs[9:]
    size_x, size_y = F.shape[:2]
    body = pl.ds(LEFT, size_y)
    low, high = RIM, RIM + size_x
    odd = odd_brick()
    pairs = []
    for x, upper in ((x_in, 1 - odd), (x_out, odd)):
        place = upper * high + (1 - upper) * (low - RIM)
        pairs.append((x.at[pl.ds(0, RIM)], L.at[pl.ds(place, RIM), body]))
        place = upper * high + (1 - upper) * (low - DEEP)
        for i in range(3):
            pairs.append(
                (x.at[pl.ds(RIM + i * DEEP, DEEP)], V.at[i, pl.ds(place, DEEP), body])
            )
        place = upper * high + (1 - upper) * (low - 1)
        pairs.append((x.at[pl.ds(RIM + 3 * DEEP, 1)], R.at[pl.ds(place, 1), body]))
    copies = copies_of(pairs, sems)
    start_all(copies)

    def spread(x, y):
        row = 8 * (x - RIM + 1)
        for side, q in enumerate((q_lo, q_hi)):
            fill(L, V, x, side, q, (), row, size_y)
            place = LEFT + size_y if side else LEFT - 1
            R[x, pl.ds(place, 1), :] = q[pl.ds(row + 7, 1), :]

    sweep(low, high, [0], spread, 16)
    for side, q in enumerate((q_lo, q_hi)):
        place = LEFT + size_y + 2 if side else LEFT - 3
        for x, near, more in ((low, low + 1, 0), (high - 1, high - 2, 8 * (size_x + 1))):
            fill_raw(L, V, x, side, q, (), 8 * (x - RIM + 1), more, size_y)
            L[near, pl.ds(place, 1), :] = q[pl.ds(more, 1), :]
    wait_all(copies)

    core = [LEFT + y for y in range(0, size_y, 8)]
    mid = [LEFT + y for y in range(RIM, size_y - RIM, 8)]
    outer = [LEFT - RIM, LEFT + size_y - RIM]
    step = functools.partial(predict, V, R, K, VS)
    sweep(low + 1, high - 1, [core[0], core[-1]], step)
    for x in (low, high - 1):
        for y in core:
            step(x, y)
    out = copies_of([(VS.at[i], star.at[i]) for i in range(3)], sems, len(copies))
    start_all(out)

    def ring(depth, cell):
        sweep(low - depth, high + depth, outer, cell)
        sweep(low - depth, low - depth + 4, mid, cell)
        sweep(high + depth - 4, high + depth, mid, cell)

    ring(3, functools.partial(advect, L, V, A, S))

    def take(x, y):
        for side, q in enumerate((q_lo, q_hi)):
            psi = q[pl.ds(8 * (x - RIM + 1) + 2, 2), :]
            place = pl.ds(LEFT + size_y + 1 if side else LEFT - 3, 2)
            A[x, place, :] = psi
            S[x, place, :] = scaled_sign(psi)

    sweep(low + 1, high - 1, [0], take, 16)
    ring(2, functools.partial(evolve, A, B, S))
    ring(1, functools.partial(evolve, B, C, S))
    ring(0, functools.partial(finish, C, S, L, M, F, size_y))
    wait_all(out)


def corner_kernel(M, z_in, z_out, *refs):
    V, L, A, S, B, C, F, new, sems = refs[7:]
    size_x, size_y = F.shape[:2]
    low, high = RIM, RIM + size_x
    early = copies_of(
        [(F.at[pl.ds(3, size_x - 6)], new.at[pl.ds(3, size_x - 6)])], sems
    )
    start_all(early)
    odd = odd_brick()
    for z, upper in ((z_in, 1 - odd), (z_out, odd)):
        place = upper * high + (1 - upper) * (low - DEEP)
        edge = upper * high + (1 - upper) * (low - 1)
        first = upper * 8
        for side in range(2):
            for k in range(DEEP):
                fill(L, V, place + k, side, z, (side,), first + k * 8, size_y)
            fill_raw(
                L, V, edge, side, z, (side,), 16 - upper * 8, 24 - upper * 24, size_y
            )

    outer = [LEFT - RIM, LEFT + size_y - RIM]

    def ends(depth, cell):
        rows = 4 if depth else 3
        for k in range(rows):
            for x in (low - depth + k, high + depth - 1 - k):
                for y in outer:
                    cell(x, y)

    ends(3, functools.partial(advect, L, V, A, S))
    ends(2, functools.partial(evolve, A, B, S))
    ends(1, functools.partial(evolve, B, C, S))
    ends(0, functools.partial(finish, C, S, L, M, F, size_y))
    late = copies_of(
        [(F.at[pl.ds(x, 3)], new.at[pl.ds(x, 3)]) for x in (0, size_x - 3)], sems, 1
    )
    start_all(late)
    wait_all(early + late)


def moved(array, axis, step):
    peers = lax.axis_size(axis)
    return lax.ppermute(array, axis, [(i, (i + step) % peers) for i in range(peers)])


def swapped(array, axis, shift):
    peers = lax.axis_size(axis)
    pairs = [(i, (((i + shift) ^ 1) - shift) % peers) for i in range(peers)]
    return lax.ppermute(array, axis, pairs)


def shards(velocity, pressure, level_set, overset, band_count, band_ids):
    size_x, size_y, size_z = level_set.shape
    plain = level_set.shape
    padded = (size_x + 2 * RIM, LEFT + size_y + 8, size_z)
    x_face = (SLABS, size_y, size_z)
    y_face = ((size_x + 2) * 8, size_z)
    marks = (size_x // BS * (size_y // BS), 8, size_z)

    x_in, x_out, y_low, y_high, V, L, R = call(
        pack_kernel,
        [("hbm", velocity), ("hbm", pressure), ("hbm", level_set)],
        [("vmem", x_face, F32)] * 2
        + [("vmem", y_face, F32)] * 2
        + [("vmem", (3,) + padded, F32), ("vmem", padded, F32), ("vmem", padded, F32)],
        "pack",
        sems=24,
    )
    q_lo = moved(y_high, "col", 1)
    q_hi = moved(y_low, "col", -1)
    x_in = swapped(x_in, "brick", 0)
    x_out = swapped(x_out, "brick", 1)
    R, K, VS, A, S, B, C, F, M = call(
        inner_kernel,
        [("vmem", V), ("vmem", L), ("hbm", pressure), ("hbm", overset)]
        + [("smem", band_count), ("hbm", band_ids), ("vmem", R)],
        [("vmem", padded, F32), ("vmem", plain, jnp.int32), ("vmem", (3,) + plain, F32)]
        + [("vmem", padded, F32)] * 4
        + [("vmem", plain, F32), ("vmem", marks, F32)],
        "inner",
        aliases={6: 0},
        scratch=[pltpu.SMEM(band_ids.shape, jnp.int32)],
        sems=3,
        flops=60 << 26,
    )
    z_in, z_out = call(
        relay_kernel,
        [("vmem", M), ("vmem", q_lo), ("vmem", q_hi)],
        [("vmem", (2, CORNER, size_z), F32)] * 2,
        "relay",
        sems=4,
    )
    z_in = swapped(z_in, "brick", 0)
    z_out = swapped(z_out, "brick", 1)
    state = [V, L, R, VS, A, S, B, C, F]
    held = [("vmem", K), ("vmem", M)] + [("vmem", a) for a in (x_in, x_out, q_lo, q_hi)]
    *state, velocity_star = call(
        edge_kernel,
        held + [("vmem", a) for a in state],
        [("vmem", a.shape, F32) for a in state] + [("hbm", velocity.shape, F32)],
        "edge",
        aliases={len(held) + i: i for i in range(len(state))},
        sems=13,
        flops=60 << 26,
    )
    V, L, R, VS, A, S, B, C, F = state
    state = [V, L, A, S, B, C, F]
    held = [("vmem", M), ("vmem", z_in), ("vmem", z_out)]
    *state, level_set_new = call(
        corner_kernel,
        held + [("vmem", a) for a in state],
        [("vmem", a.shape, F32) for a in state] + [("hbm", plain, F32)],
        "corner",
        aliases={len(held) + i: i for i in range(len(state))},
        sems=3,
    )
    return (velocity_star, level_set_new)


def solution(mesh):
    return jax.shard_map(
        shards,
        mesh=mesh,
        in_specs=(
            P(None, "brick", "col", None),
            P("brick", "col", None),
            P("brick", "col", None),
            P("brick", "col", None),
            P("brick", "col"),
            P("brick", "col", None),
        ),
        out_specs=(P(None, "brick", "col", None), P("brick", "col", None)),
        check_vma=False,
    )
```

```python
import functools

import jax
import jax.numpy as jnp
from jax import lax
from jax.experimental import pallas as pl
from jax.experimental.pallas import tpu as pltpu
from jax.sharding import PartitionSpec as P

BS = 16
REINIT = 3
MAXB = 16
RIM = 4
DEEP = 3
SLABS = RIM + 3 * DEEP + 1
CORNER = 32
LEFT = 8
UNROLL = 120

DT = 0.1
VISC = 0.5
DT_SET = 0.2
TAU = 0.5

F32 = jnp.float32
ANY = pl.BlockSpec(memory_space=pl.ANY)
VM = pl.BlockSpec(memory_space=pltpu.VMEM)
SM = pl.BlockSpec(memory_space=pltpu.SMEM)


def call(kernel, args, outs, name, aliases=None, sems=0, flops=1 << 20, scratch=()):
    specs = {"vmem": VM, "hbm": ANY, "smem": SM}
    spaces = {"vmem": pltpu.VMEM, "hbm": pltpu.HBM}
    operands = [
        pltpu.with_memory_space_constraint(a, spaces[k]) if k in spaces else a for k, a in args
    ]
    shapes = [
        pltpu.VMEM(s, t) if k == "vmem" else jax.ShapeDtypeStruct(s, t) for k, s, t in outs
    ]
    return pl.pallas_call(
        kernel,
        out_shape=shapes,
        in_specs=[specs[k] for k, _ in args],
        out_specs=[specs[k] for k, _, _ in outs],
        input_output_aliases=aliases or {},
        scratch_shapes=list(scratch) + [pltpu.SemaphoreType.DMA((sems,))],
        cost_estimate=pl.CostEstimate(
            flops=flops, bytes_accessed=4 << 20, transcendentals=0
        ),
        compiler_params=pltpu.CompilerParams(vmem_limit_bytes=8 << 20),
        name=name,
    )(*operands)


def copies_of(pairs, sems, first=0):
    return [
        pltpu.make_async_copy(s, d, sems.at[first + i]) for i, (s, d) in enumerate(pairs)
    ]


def start_all(copies):
    for copy in copies:
        copy.start()


def wait_all(copies):
    for copy in copies:
        copy.wait()


def sweep(low, high, tiles, cell, limit=UNROLL):
    rows = high - low
    group = max(g for g in range(1, rows + 1) if rows % g == 0 and g * len(tiles) <= limit)

    def some(i, carry):
        for k in range(group):
            for y in tiles:
                cell(low + i * group + k, y)
        return carry

    if group == rows:
        some(0, 0)
    else:
        lax.fori_loop(0, rows // group, some, 0)


def odd_brick():
    return lax.axis_index("brick") % 2


def pack_kernel(vel, press, level, x_in, x_out, y_lo, y_hi, V, L, R, sems):
    size_x, size_y = level.shape[:2]
    odd = odd_brick()
    inner = pl.ds(RIM, size_x)

    def part(first, count):
        rows, place = pl.ds(first, count), pl.ds(LEFT + first, count)
        return [
            (level.at[:, rows], L.at[inner, place]),
            (vel.at[:, :, rows], V.at[:, inner, place]),
            (press.at[:, rows], R.at[inner, place]),
        ]

    strips = part(0, 8) + part(size_y - 8, 8)
    rest = []
    for out, high in ((x_in, 1 - odd), (x_out, odd)):
        def rows(n):
            return pl.ds(high * (size_x - n), n)

        rest.append((level.at[rows(RIM)], out.at[pl.ds(0, RIM)]))
        for i in range(3):
            rest.append((vel.at[i, rows(DEEP)], out.at[pl.ds(RIM + i * DEEP, DEEP)]))
        rest.append((press.at[rows(1)], out.at[pl.ds(RIM + 3 * DEEP, 1)]))
    rest += part(8, size_y - 16)[:2]
    strips = copies_of(strips, sems)
    rest = copies_of(rest, sems, len(strips))
    start_all(strips + rest)

    def put(out, row, ref, x, y, n, *lead):
        out[pl.ds(row, n), :] = ref[(*lead, x, pl.ds(LEFT + y, n), slice(None))]

    def gather(out, high, x, y):
        row = 8 * (x - RIM + 1)
        near = size_y - 1 if high else 0
        put(out, row, L, x, size_y - 2 if high else 0, 2)
        first = size_y - 7 if high else -1
        psi = advected(L, V, x, LEFT + first)
        place = (size_y - 3 if high else 1) - first
        out[pl.ds(row + 2, 2), :] = psi[place : place + 2]
        for i in range(3):
            put(out, row + 4 + i, V, x, near, 1, i)
        put(out, row + 7, R, x, near, 1)

    for high, out in enumerate((y_lo, y_hi)):
        wait_all(strips[3 * high : 3 * high + 3])
        sweep(RIM, RIM + size_x, [0], functools.partial(gather, out, high), 32)
        for x, near, more in (
            (RIM, RIM + 1, 0),
            (RIM + size_x - 1, RIM + size_x - 2, 8 * (size_x + 1)),
        ):
            put(out, 8 * (x - RIM + 1) + 2, L, x, size_y - 4 if high else 2, 2)
            put(out, more, L, near, size_y - 3 if high else 2, 1)
            for i in range(3):
                put(out, more + 1 + 2 * i, V, x, size_y - 3 if high else 1, 2, i)
    wait_all(rest)


def fill(L, V, x, side, ref, lead, row, size_y):
    place = LEFT + size_y if side else LEFT - 2
    L[x, pl.ds(place, 2), :] = ref[(*lead, pl.ds(row, 2), slice(None))]
    place = LEFT + size_y if side else LEFT - 1
    for i in range(3):
        V[i, x, pl.ds(place, 1), :] = ref[(*lead, pl.ds(row + 4 + i, 1), slice(None))]


def fill_raw(L, V, x, side, ref, lead, row, more, size_y):
    place = LEFT + size_y + 2 if side else LEFT - 4
    L[x, pl.ds(place, 2), :] = ref[(*lead, pl.ds(row + 2, 2), slice(None))]
    place = LEFT + size_y + 1 if side else LEFT - 3
    for i in range(3):
        V[i, x, pl.ds(place, 2), :] = ref[(*lead, pl.ds(more + 1 + 2 * i, 2), slice(None))]


def relay_kernel(after, q_lo, q_hi, z_in, z_out, sems):
    rows = q_lo.shape[0]
    odd = odd_brick()
    pairs = []
    for out, high in ((z_in, 1 - odd), (z_out, odd)):
        start = pl.multiple_of(high * (rows - CORNER), 8)
        for side, q in enumerate((q_lo, q_hi)):
            pairs.append((q.at[pl.ds(start, CORNER)], out.at[side]))
    copies = copies_of(pairs, sems)
    start_all(copies)
    wait_all(copies)


def turn(value):
    return pltpu.roll(value, 1, 1), pltpu.roll(value, value.shape[1] - 1, 1)


def tile(ref, x, y, *lead):
    return ref[(*lead, x, pl.ds(y, 8), slice(None))]


def predict(V, R, K, VS, x, y):
    kinds = tile(K, x - RIM, y - LEFT)
    rm, rp = turn(tile(R, x, y))
    grads = (
        tile(R, x + 1, y) - tile(R, x - 1, y),
        tile(R, x, y + 1) - tile(R, x, y - 1),
        rp - rm,
    )
    speed = [tile(V, x, y, i) for i in range(3)]
    for i in range(3):
        zm, zp = turn(speed[i])
        plus = (tile(V, x + 1, y, i), tile(V, x, y + 1, i), zp)
        minus = (tile(V, x - 1, y, i), tile(V, x, y - 1, i), zm)
        total = (plus[0] + minus[0]) + (plus[1] + minus[1]) + (plus[2] + minus[2])
        conv = (
            speed[0] * (plus[0] - minus[0])
            + speed[1] * (plus[1] - minus[1])
            + speed[2] * (plus[2] - minus[2])
        )
        pred = (1.0 - 6.0 * DT * VISC) * speed[i] + (
            DT * VISC * total - 0.5 * DT * (conv + grads[i])
        )
        mean = total * (1.0 / 6.0)
        VS[i, x - RIM, pl.ds(y - LEFT, 8), :] = jnp.where(
            kinds == 1, mean, jnp.where(kinds == 2, 0.0, pred)
        )


def advected(L, V, x, y):
    c = tile(L, x, y)
    zm, zp = turn(c)
    v = [tile(V, x, y, i) for i in range(3)]
    flux = None
    for u, m, p in (
        (v[0], tile(L, x - 1, y), tile(L, x + 1, y)),
        (v[1], tile(L, x, y - 1), tile(L, x, y + 1)),
        (v[2], zm, zp),
    ):
        term = u * jnp.where(u > 0, c - m, p - c)
        flux = term if flux is None else flux + term
    return c - DT_SET * flux


def scaled_sign(psi):
    return (TAU * psi) * lax.rsqrt(psi * psi + 1.0)


def advect(L, V, A, S, x, y):
    psi = advected(L, V, x, y)
    A[x, pl.ds(y, 8), :] = psi
    S[x, pl.ds(y, 8), :] = scaled_sign(psi)


def evolved(ref, S, x, y):
    c = tile(ref, x, y)
    s = tile(S, x, y)
    zm, zp = turn(c)
    up = s > 0
    g = None
    for m, p in (
        (tile(ref, x - 1, y), tile(ref, x + 1, y)),
        (tile(ref, x, y - 1), tile(ref, x, y + 1)),
        (zm, zp),
    ):
        low = c - jnp.minimum(jnp.minimum(m, p), c)
        high = jnp.maximum(jnp.maximum(m, p), c) - c
        d = jnp.where(up, low, high)
        g = d * d if g is None else g + d * d
    return c - s * (g * lax.rsqrt(g + 1e-30) - 1.0)


def evolve(source, target, S, x, y):
    target[x, pl.ds(y, 8), :] = evolved(source, S, x, y)


def finish(source, S, L, M, F, size_y, x, y):
    new = evolved(source, S, x, y)
    y0 = max(y, LEFT)
    y1 = min(y + 8, LEFT + size_y)
    wide = size_y // BS
    first = (y0 - LEFT) // BS
    last = (y1 - 1 - LEFT) // BS
    mark = M[(x - RIM) // BS * wide + first]
    if first != last:
        edge = LEFT + last * BS - y
        rows = lax.broadcasted_iota(jnp.int32, mark.shape, 0)
        mark = jnp.where(rows < edge, mark, M[(x - RIM) // BS * wide + last])
    value = jnp.where(mark > 0.5, new, tile(L, x, y))
    F[x - RIM, pl.ds(y0 - LEFT, y1 - y0), :] = value[y0 - y : y1 - y]


def inner_kernel(
    V, L, press, overset, count, band_ids, _, R, K, VS, A, S, B, C, F, M, ids, sems
):
    size_x, size_y, size_z = F.shape
    middle = size_y - 16
    named = copies_of([(band_ids, ids)], sems)
    later = copies_of(
        [
            (press.at[:, pl.ds(8, middle)], R.at[pl.ds(RIM, size_x), pl.ds(LEFT + 8, middle)]),
            (overset, K),
        ],
        sems,
        1,
    )
    start_all(named + later)
    core = [LEFT + y for y in range(0, size_y, 8)]
    mid = [LEFT + y for y in range(RIM, size_y - RIM, 8)]
    low, high = RIM, RIM + size_x
    sweep(low + 1, high - 1, core, functools.partial(advect, L, V, A, S))
    sweep(low + 2, high - 2, core, functools.partial(evolve, A, B, S))
    sweep(low + 3, high - 3, core, functools.partial(evolve, B, C, S))

    wait_all(named)
    wide = size_y // BS
    deep = size_z // BS
    lane = lax.broadcasted_iota(jnp.int32, (8, size_z), 1) // BS
    marks = [jnp.zeros((8, size_z), jnp.bool_) for _ in range(size_x // BS * wide)]
    held = count[0, 0]
    for s in range(MAXB):
        block = jnp.where(s < held, ids[0, 0, s], -1)
        marks = [m | (lane == block - k * deep) for k, m in enumerate(marks)]
    for k, m in enumerate(marks):
        M[k] = m.astype(F32)

    sweep(low + 4, high - 4, mid, functools.partial(finish, C, S, L, M, F, size_y))
    wait_all(later)
    sweep(low + 1, high - 1, core[1:-1], functools.partial(predict, V, R, K, VS))


def edge_kernel(
    K, M, x_in, x_out, q_lo, q_hi, *refs
):
    V, L, R, VS, A, S, B, C, F, star, sems = refs[9:]
    size_x, size_y = F.shape[:2]
    body = pl.ds(LEFT, size_y)
    low, high = RIM, RIM + size_x
    odd = odd_brick()
    pairs = []
    for x, upper in ((x_in, 1 - odd), (x_out, odd)):
        place = upper * high + (1 - upper) * (low - RIM)
        pairs.append((x.at[pl.ds(0, RIM)], L.at[pl.ds(place, RIM), body]))
        place = upper * high + (1 - upper) * (low - DEEP)
        for i in range(3):
            pairs.append(
                (x.at[pl.ds(RIM + i * DEEP, DEEP)], V.at[i, pl.ds(place, DEEP), body])
            )
        place = upper * high + (1 - upper) * (low - 1)
        pairs.append((x.at[pl.ds(RIM + 3 * DEEP, 1)], R.at[pl.ds(place, 1), body]))
    copies = copies_of(pairs, sems)
    start_all(copies)

    def spread(x, y):
        row = 8 * (x - RIM + 1)
        for side, q in enumerate((q_lo, q_hi)):
            fill(L, V, x, side, q, (), row, size_y)
            place = LEFT + size_y if side else LEFT - 1
            R[x, pl.ds(place, 1), :] = q[pl.ds(row + 7, 1), :]

    sweep(low, high, [0], spread, 32)
    for side, q in enumerate((q_lo, q_hi)):
        place = LEFT + size_y + 2 if side else LEFT - 3
        for x, near, more in ((low, low + 1, 0), (high - 1, high - 2, 8 * (size_x + 1))):
            fill_raw(L, V, x, side, q, (), 8 * (x - RIM + 1), more, size_y)
            L[near, pl.ds(place, 1), :] = q[pl.ds(more, 1), :]
    wait_all(copies)

    core = [LEFT + y for y in range(0, size_y, 8)]
    mid = [LEFT + y for y in range(RIM, size_y - RIM, 8)]
    outer = [LEFT - RIM, LEFT + size_y - RIM]
    step = functools.partial(predict, V, R, K, VS)
    sweep(low + 1, high - 1, [core[0], core[-1]], step)
    for x in (low, high - 1):
        for y in core:
            step(x, y)
    out = copies_of([(VS.at[i], star.at[i]) for i in range(3)], sems, len(copies))
    start_all(out)

    def ring(depth, cell):
        sweep(low - depth, high + depth, outer, cell)
        sweep(low - depth, low - depth + 4, mid, cell)
        sweep(high + depth - 4, high + depth, mid, cell)

    ring(3, functools.partial(advect, L, V, A, S))

    def take(x, y):
        for side, q in enumerate((q_lo, q_hi)):
            psi = q[pl.ds(8 * (x - RIM + 1) + 2, 2), :]
            place = pl.ds(LEFT + size_y + 1 if side else LEFT - 3, 2)
            A[x, place, :] = psi
            S[x, place, :] = scaled_sign(psi)

    sweep(low + 1, high - 1, [0], take, 32)
    ring(2, functools.partial(evolve, A, B, S))
    ring(1, functools.partial(evolve, B, C, S))
    ring(0, functools.partial(finish, C, S, L, M, F, size_y))
    wait_all(out)


def corner_kernel(M, z_in, z_out, *refs):
    V, L, A, S, B, C, F, new, sems = refs[7:]
    size_x, size_y = F.shape[:2]
    low, high = RIM, RIM + size_x
    early = copies_of(
        [(F.at[pl.ds(3, size_x - 6)], new.at[pl.ds(3, size_x - 6)])], sems
    )
    start_all(early)
    odd = odd_brick()
    for z, upper in ((z_in, 1 - odd), (z_out, odd)):
        place = upper * high + (1 - upper) * (low - DEEP)
        edge = upper * high + (1 - upper) * (low - 1)
        first = upper * 8
        for side in range(2):
            for k in range(DEEP):
                fill(L, V, place + k, side, z, (side,), first + k * 8, size_y)
            fill_raw(
                L, V, edge, side, z, (side,), 16 - upper * 8, 24 - upper * 24, size_y
            )

    outer = [LEFT - RIM, LEFT + size_y - RIM]

    def ends(depth, cell):
        rows = 4 if depth else 3
        for k in range(rows):
            for x in (low - depth + k, high + depth - 1 - k):
                for y in outer:
                    cell(x, y)

    ends(3, functools.partial(advect, L, V, A, S))
    ends(2, functools.partial(evolve, A, B, S))
    ends(1, functools.partial(evolve, B, C, S))
    ends(0, functools.partial(finish, C, S, L, M, F, size_y))
    late = copies_of(
        [(F.at[pl.ds(x, 3)], new.at[pl.ds(x, 3)]) for x in (0, size_x - 3)], sems, 1
    )
    start_all(late)
    wait_all(early + late)


def moved(array, axis, step):
    peers = lax.axis_size(axis)
    return lax.ppermute(array, axis, [(i, (i + step) % peers) for i in range(peers)])


def swapped(array, axis, shift):
    peers = lax.axis_size(axis)
    pairs = [(i, (((i + shift) ^ 1) - shift) % peers) for i in range(peers)]
    return lax.ppermute(array, axis, pairs)


def shards(velocity, pressure, level_set, overset, band_count, band_ids):
    size_x, size_y, size_z = level_set.shape
    plain = level_set.shape
    padded = (size_x + 2 * RIM, LEFT + size_y + 8, size_z)
    x_face = (SLABS, size_y, size_z)
    y_face = ((size_x + 2) * 8, size_z)
    marks = (size_x // BS * (size_y // BS), 8, size_z)

    x_in, x_out, y_low, y_high, V, L, R = call(
        pack_kernel,
        [("hbm", velocity), ("hbm", pressure), ("hbm", level_set)],
        [("vmem", x_face, F32)] * 2
        + [("vmem", y_face, F32)] * 2
        + [("vmem", (3,) + padded, F32), ("vmem", padded, F32), ("vmem", padded, F32)],
        "pack",
        sems=24,
    )
    q_lo = moved(y_high, "col", 1)
    q_hi = moved(y_low, "col", -1)
    x_in = swapped(x_in, "brick", 0)
    x_out = swapped(x_out, "brick", 1)
    R, K, VS, A, S, B, C, F, M = call(
        inner_kernel,
        [("vmem", V), ("vmem", L), ("hbm", pressure), ("hbm", overset)]
        + [("smem", band_count), ("hbm", band_ids), ("vmem", R)],
        [("vmem", padded, F32), ("vmem", plain, jnp.int32), ("vmem", (3,) + plain, F32)]
        + [("vmem", padded, F32)] * 4
        + [("vmem", plain, F32), ("vmem", marks, F32)],
        "inner",
        aliases={6: 0},
        scratch=[pltpu.SMEM(band_ids.shape, jnp.int32)],
        sems=3,
        flops=60 << 26,
    )
    z_in, z_out = call(
        relay_kernel,
        [("vmem", M), ("vmem", q_lo), ("vmem", q_hi)],
        [("vmem", (2, CORNER, size_z), F32)] * 2,
        "relay",
        sems=4,
    )
    z_in = swapped(z_in, "brick", 0)
    z_out = swapped(z_out, "brick", 1)
    state = [V, L, R, VS, A, S, B, C, F]
    held = [("vmem", K), ("vmem", M)] + [("vmem", a) for a in (x_in, x_out, q_lo, q_hi)]
    *state, velocity_star = call(
        edge_kernel,
        held + [("vmem", a) for a in state],
        [("vmem", a.shape, F32) for a in state] + [("hbm", velocity.shape, F32)],
        "edge",
        aliases={len(held) + i: i for i in range(len(state))},
        sems=13,
        flops=60 << 26,
    )
    V, L, R, VS, A, S, B, C, F = state
    state = [V, L, A, S, B, C, F]
    held = [("vmem", M), ("vmem", z_in), ("vmem", z_out)]
    *state, level_set_new = call(
        corner_kernel,
        held + [("vmem", a) for a in state],
        [("vmem", a.shape, F32) for a in state] + [("hbm", plain, F32)],
        "corner",
        aliases={len(held) + i: i for i in range(len(state))},
        sems=3,
    )
    return (velocity_star, level_set_new)


def solution(mesh):
    return jax.shard_map(
        shards,
        mesh=mesh,
        in_specs=(
            P(None, "brick", "col", None),
            P("brick", "col", None),
            P("brick", "col", None),
            P("brick", "col", None),
            P("brick", "col"),
            P("brick", "col", None),
        ),
        out_specs=(P(None, "brick", "col", None), P("brick", "col", None)),
        check_vma=False,
    )
```
